512 devices in a mesh: section: 16 (over y_hi, x), dp: 32 (over y_lo, z, core).
Axes of the slice: x: 4, y: 8 (y_hi: 4, y_lo: 2; y = y_hi * 2 + y_lo), z: 8, core: 2. Of those that a mesh axis runs over, the one named last changes fastest.
Arguments:
- x_down: bfloat16 [32, 8, 8, 5120], P('dp'), may hold values from -6 to 6
- x_up: bfloat16 [32, 8, 8, 5120], P('dp'), may hold values from -6 to 6
- cot_down: bfloat16 [32, 8, 8, 5120], P('dp'), may hold values from -6 to 6
- cot_up: bfloat16 [32, 8, 8, 5120], P('dp'), may hold values from -6 to 6
- gain: bfloat16 [16, 5120], P('section'), may hold values from 0.25 to 1.75
- w_a: bfloat16 [16, 32, 5120], P('section'), may hold values from -0.078125 to 0.078125
- w_b: bfloat16 [16, 32, 5120], P('section'), may hold values from -1 to 1
Outputs:
- gain_gradient: float32 [16, 5120], P('section')
- grad_a: float32 [16, 32, 5120], P('section')
- grad_b: float32 [16, 32, 5120], P('section')
The draws below stay inside these ranges and needn't reach their ends.
All inputs are finite; a program needn't handle non-finite values.
Results may differ from the reference program's by a relative error of at most 0.035.
Values may be sent and summed in bfloat16 or wider, within the bound.
A program may use at most 64 MiB of HBM per device.

```python
import jax
import jax.numpy as jnp
from jax import lax

D = 5120
R = 32
MB = 8
ROWS = 8
SECTIONS = 16
REPLICAS = 32
N_SECTION = 16


def shard_levels(key, dims, shards, smallest, high):
    def one(axis_at, blocks):
        heights = jax.random.uniform(jax.random.fold_in(jax.random.fold_in(key, 6), axis_at), (blocks,), jnp.float32, smallest / len(shards), high / len(shards))
        return jnp.repeat(jnp.exp(heights), dims[axis_at] // blocks).reshape((-1,) + (1,) * (len(dims) - axis_at - 1))

    loudness = one(*shards[0])
    for cut in shards[1:]:
        loudness = loudness * one(*cut)
    return loudness


def scatter_about(stream_key, extent, spread, limit, pieces=(), held_as=jnp.bfloat16):
    values = jax.random.normal(stream_key, extent, jnp.float32) * spread
    if len(pieces) > 0:
        values = shard_levels(stream_key, extent, pieces, -0.22, 0.18) * values
    return jnp.clip(values, min=-limit, max=limit).astype(held_as)


def setup_inputs(seed: int = 0) -> dict:
    splits = jax.random.split(jax.random.key(seed), 8)
    x_down = scatter_about(splits[0], (REPLICAS, MB, ROWS, D), 1.0, 6.0, ((0, 32),))
    x_up = scatter_about(splits[1], (REPLICAS, MB, ROWS, D), 1.0, 6.0, ((0, 32),))
    cot_down = scatter_about(splits[2], (REPLICAS, MB, ROWS, D), 1.0, 6.0, ((0, 32),))
    cot_up = scatter_about(splits[3], (REPLICAS, MB, ROWS, D), 1.0, 6.0, ((0, 32),))
    gain = jnp.clip(1.0 + 0.15 * jax.random.normal(splits[4], (SECTIONS, D), jnp.float32), 0.25, 1.75).astype(jnp.bfloat16)
    w_a = scatter_about(splits[5], (SECTIONS, R, D), D ** -0.5, 0.078125, ((0, 16),))
    w_b = scatter_about(splits[6], (SECTIONS, R, D), R ** -0.5, 1.0, ((0, 16),))
    return dict(x_down=x_down, x_up=x_up, cot_down=cot_down, cot_up=cot_up, gain=gain, w_a=w_a, w_b=w_b)


def section_forward(x, gain, w_a, w_b):
    xf = x.astype(jnp.float32)
    centered_input = xf - lax.optimization_barrier(jnp.mean(xf, axis=-1, keepdims=True))
    inverse_deviation = lax.rsqrt(lax.optimization_barrier(jnp.mean(centered_input * centered_input, axis=-1, keepdims=True)) + 1e-05)
    standardized_input = centered_input * inverse_deviation
    normalized_output = (standardized_input * gain.astype(jnp.float32)).astype(jnp.bfloat16)
    hidden = lax.dot_general(normalized_output, w_a, (((1,), (1,)), ((), ())), preferred_element_type=jnp.float32)
    act = jax.nn.gelu(hidden).astype(jnp.bfloat16)
    return (xf + jnp.dot(act, w_b, preferred_element_type=jnp.float32)).astype(jnp.bfloat16)

def section_backward(x, grad_y, gain, w_a, w_b):
    xf = x.astype(jnp.float32)
    centered_input = xf - lax.optimization_barrier(jnp.mean(xf, axis=-1, keepdims=True))
    inverse_deviation = lax.rsqrt(lax.optimization_barrier(jnp.mean(centered_input * centered_input, axis=-1, keepdims=True)) + 1e-05)
    standardized_input = centered_input * inverse_deviation
    gain_float = gain.astype(jnp.float32)
    normalized_output = (standardized_input * gain_float).astype(jnp.bfloat16)
    hidden = lax.dot_general(normalized_output, w_a, (((1,), (1,)), ((), ())), preferred_element_type=jnp.float32)
    act = jax.nn.gelu(hidden).astype(jnp.bfloat16)
    grad_b = lax.dot_general(act, grad_y, (((0,), (0,)), ((), ())), preferred_element_type=jnp.float32)
    grad_act = lax.dot_general(grad_y, w_b, (((1,), (1,)), ((), ())), preferred_element_type=jnp.float32)
    grad_hidden = jax.vjp(jax.nn.gelu, hidden)[1](grad_act)[0].astype(jnp.bfloat16)
    grad_a = lax.dot_general(grad_hidden, normalized_output, (((0,), (0,)), ((), ())), preferred_element_type=jnp.float32)
    normalized_gradient = jnp.dot(grad_hidden, w_a, preferred_element_type=jnp.float32)
    gain_gradient = lax.optimization_barrier(jnp.sum(normalized_gradient * standardized_input, axis=0))
    standardized_gradient = normalized_gradient * gain_float
    inner_product = standardized_gradient - lax.optimization_barrier(jnp.mean(standardized_gradient, axis=-1, keepdims=True)) - standardized_input * lax.optimization_barrier(jnp.mean(standardized_gradient * standardized_input, axis=-1, keepdims=True))
    grad_x = (grad_y.astype(jnp.float32) + inverse_deviation * inner_product).astype(jnp.bfloat16)
    return (grad_x, gain_gradient, grad_a, grad_b)

def reference(x_down, x_up, cot_down, cot_up, gain, w_a, w_b):
    width = x_down.shape[-1]
    acts = jnp.concatenate([x_down.reshape(-1, width), x_up.reshape(-1, width)], axis=0)
    grad_y = jnp.concatenate([cot_down.reshape(-1, width), cot_up.reshape(-1, width)], axis=0)
    kept = []
    for level in range(N_SECTION):
        kept.append(acts)
        acts = section_forward(acts, gain[level], w_a[level], w_b[level])
    gains_out = [None] * N_SECTION
    a_out = [None] * N_SECTION
    b_out = [None] * N_SECTION
    for level in range(N_SECTION - 1, -1, -1):
        grad_y, gains_out[level], a_out[level], b_out[level] = section_backward(kept[level], grad_y, gain[level], w_a[level], w_b[level])
    return (jnp.stack(gains_out), jnp.stack(a_out), jnp.stack(b_out))
```

```python
import jax
import jax.numpy as jnp
from jax import lax
from jax.experimental import pallas as pl
from jax.experimental.pallas import tpu as pltpu
from jax.sharding import PartitionSpec as P

F32, BF16 = jnp.float32, jnp.bfloat16
S, R, H, LANES = 16, 32, 16, 512
MBS = 8
MESH = pl.DeviceIdType.MESH
NT = (((1,), (1,)), ((), ()))
TN = (((0,), (0,)), ((), ()))


def dot(a, b, dims=(((1,), (0,)), ((), ()))):
    return lax.dot_general(a, b, dims, preferred_element_type=F32)


def gelu_pair(h):
    k = 0.7978845608028654
    t = jnp.tanh(k * (h + 0.044715 * h * h * h))
    act = 0.5 * h * (1.0 + t)
    slope = 0.5 * (1.0 + t) + 0.5 * h * (1.0 - t * t) * (k * (1.0 + 3 * 0.044715 * h * h))
    return act, slope


def halves(m):
    hi = m.astype(BF16)
    return hi, (m - hi.astype(F32)).astype(BF16)


def chain_kernel(rows_ref, w_ref, msg_ref, sc_ref, mn, kt, raw):
    width = rows_ref.shape[1]
    gw_ref, wb_ref = w_ref.at[0:LANES], w_ref.at[LANES:]
    def block(b, _):
        cols = pl.ds(pl.multiple_of(b * 256, 256), 256)
        raw[b] = dot(wb_ref[...], gw_ref[cols, :], NT)
        raw[b + 2] = dot(wb_ref[...], wb_ref[cols, :], NT)
        return 0
    lax.fori_loop(0, 2, block, 0)
    for b in range(4):
        for s in range(S):
            part = raw[b, s * R:(s + 1) * R, :]
            hi, lo = halves(part)
            mn[s, 0:R, b * 256:(b + 1) * 256] = hi
            mn[s, R:2 * R, b * 256:(b + 1) * 256] = lo
    for b in range(2):
        for t in range(4):
            for u in range(2):
                tile = raw[b, t * 128:(t + 1) * 128, u * 128:(u + 1) * 128].T
                hi, lo = halves(tile)
                for q in range(4):
                    s = (b * 2 + u) * 4 + q
                    kt[s, 0:R, t * 128:(t + 1) * 128] = hi[q * R:(q + 1) * R]
                    kt[s, R:2 * R, t * 128:(t + 1) * 128] = lo[q * R:(q + 1) * R]
    rows = rows_ref[...]
    x0 = rows[0:8].astype(F32)
    lhs = jnp.concatenate([rows, jnp.ones_like(rows)], axis=0)
    pg = dot(lhs, gw_ref[...], NT)
    pb = dot(lhs, wb_ref[...], NT)
    u, v, c = pg[0:8], pb[0:8], pb[8:16]
    gws, wbs = pg[16:17], pb[16:17]
    mu = jnp.sum(x0, axis=1, keepdims=True) / width
    cen = x0 - mu
    q = jnp.sum(cen * cen, axis=1, keepdims=True)
    lane = lax.broadcasted_iota(jnp.int32, (8, LANES), 1)
    hid, slope, rstds, mus, vs, acts = [], [], [], [], [], []
    for s in range(S):
        sl = slice(s * R, (s + 1) * R)
        rstd = lax.rsqrt(q / width + 1e-5)
        h = rstd * (u[:, sl] - mu * gws[:, sl])
        a, g = gelu_pair(h)
        a16 = a.astype(BF16)
        af = a16.astype(F32)
        hid.append(h); slope.append(g); rstds.append(rstd); mus.append(mu); vs.append(v); acts.append(af)
        if s < S - 1:
            step = dot(jnp.concatenate([a16, a16], axis=1), mn[s])
            v_new = v + step[:, LANES:]
            u = u + step[:, :LANES]
            tot = jnp.sum(af * wbs[:, sl], axis=1, keepdims=True)
            q = q + jnp.sum(af * (v[:, sl] + v_new[:, sl] - (2.0 * mu) * wbs[:, sl]), axis=1, keepdims=True) - tot * tot / width
            q = jnp.maximum(q, 0.0)
            mu = mu + tot / width
            v = v_new
    fs, cs, es = [None] * S, [None] * S, [None] * S
    cc = jnp.zeros_like(mu)
    ee = jnp.zeros_like(mu)
    for j in range(S - 1, -1, -1):
        sl = slice(j * R, (j + 1) * R)
        cs[j], es[j] = cc, ee
        dh = (c[:, sl] * slope[j]).astype(BF16)
        dhf = dh.astype(F32)
        rstd = rstds[j]
        a_j = rstd * jnp.sum(dhf * gws[:, sl], axis=1, keepdims=True) / width
        c_j = rstd * rstd * jnp.sum(dhf * hid[j], axis=1, keepdims=True) / width
        e_j = a_j - c_j * mus[j]
        fs[j] = rstd * dhf
        if j > 0:
            step = dot(jnp.concatenate([dh, dh], axis=1), kt[j])
            c = c + rstd * step - c_j * vs[j] - e_j * wbs
        cc = cc + c_j
        ee = ee + e_j
    act_all = jnp.concatenate(acts, axis=1)
    d_all = jnp.concatenate([acts[i] * cs[i] for i in range(S - 1)] + [acts[S - 1]], axis=1)
    f_all = jnp.concatenate(fs, axis=1)
    lane_sc = lax.broadcasted_iota(jnp.int32, (8, 128), 1)
    for s in range(S):
        z = jnp.where(lane < s * R, act_all, d_all)
        z = jnp.concatenate([z[:, :LANES - R], acts[s]], axis=1)
        f = jnp.concatenate([fs[s], f_all[:, R:]], axis=1)
        msg_ref[s] = jnp.concatenate([z, f], axis=0).astype(BF16)
        sc_ref[s] = jnp.where(lane_sc == 0, mus[s], jnp.where(lane_sc == 1, cs[s], es[s]))


def chain(rows, w):
    width = rows.shape[1]
    return pl.pallas_call(
        chain_kernel,
        out_shape=(jax.ShapeDtypeStruct((S, 16, LANES), BF16), jax.ShapeDtypeStruct((S, 8, 128), F32)),
        in_specs=[pl.BlockSpec(memory_space=pltpu.VMEM)] * 2,
        out_specs=(pl.BlockSpec(memory_space=pltpu.VMEM),) * 2,
        scratch_shapes=[
            pltpu.VMEM((S, 2 * R, 2 * LANES), BF16),
            pltpu.VMEM((S, 2 * R, LANES), BF16),
            pltpu.VMEM((4, LANES, 256), F32),
        ],
        compiler_params=pltpu.CompilerParams(vmem_limit_bytes=56 * 2**20),
    )(rows, w)


def final_kernel(msg_ref, sc_ref, xd, xu, cd, cu, w_ref, out_ref):
    gw_ref, wb_ref = w_ref.at[0:LANES], w_ref.at[LANES:]
    s = lax.axis_index("section")
    z = jnp.concatenate([msg_ref[i, 0:8] for i in range(S)], axis=0)
    f = jnp.concatenate([msg_ref[i, 8:16] for i in range(S)], axis=0)
    sc = jnp.concatenate([sc_ref[i] for i in range(S)], axis=0)
    mu, cc, ee = sc[:, 0:1], sc[:, 1:2], sc[:, 2:3]
    lane = lax.broadcasted_iota(jnp.int32, z.shape, 1)
    zero = jnp.zeros_like(z)
    zx = jnp.where(lane < s * R, z, zero)
    zd = jnp.where((lane >= s * R) & (lane < LANES - R), z, zero)
    fd = jnp.where(lane >= (s + 1) * R, f, zero)
    act, fs = z[:, LANES - R:], f[:, :R]
    x = jnp.concatenate([xd[...], xu[...]], axis=0).astype(F32) + dot(zx, wb_ref[...])
    dy = jnp.concatenate([cd[...], cu[...]], axis=0).astype(F32) + dot(fd, gw_ref[...]) - dot(zd, wb_ref[...])
    dy = dy - cc * x - ee
    out_ref[0, 0:R] = dot(fs, (x - mu).astype(BF16), TN).astype(BF16)
    out_ref[0, R:2 * R] = dot(act, dy.astype(BF16), TN).astype(BF16)


def final(msg, sc, xd, xu, cd, cu, w, step=640):
    width = xd.shape[1]
    n = width // step
    col = lambda rows: pl.BlockSpec((rows, step), lambda i: (0, i))
    whole = lambda shape: pl.BlockSpec(shape, lambda i: (0,) * len(shape))
    return pl.pallas_call(
        final_kernel,
        grid=(n,),
        out_shape=jax.ShapeDtypeStruct((n, 2 * R, step), BF16),
        in_specs=[whole(msg.shape), whole(sc.shape)] + [col(xd.shape[0])] * 4 + [col(w.shape[0])],
        out_specs=pl.BlockSpec((1, 2 * R, step), lambda i: (i, 0, 0)),
        compiler_params=pltpu.CompilerParams(vmem_limit_bytes=56 * 2**20),
    )(msg, sc, xd, xu, cd, cu, w)


def place():
    me, dp = lax.axis_index("section"), lax.axis_index("dp")
    deep = lax.axis_size("dp") // 4
    core = lax.rem(dp, 2)
    z = lax.rem(dp // 2, deep)
    y_lo = dp // (2 * deep)
    return me, me // 4, lax.rem(me, 4), y_lo, z, core, deep


def greet(partners):
    barrier = pltpu.get_barrier_semaphore()
    for partner in partners:
        pl.semaphore_signal(barrier, inc=1, device_id=partner, device_id_type=MESH)
    pl.semaphore_wait(barrier, len(partners))


class Units:
    def __init__(self, buf, send, recv):
        self.buf, self.send, self.recv = buf, send, recv
        self.pending = []
        self.next = 0

    def view(self, kind, sec, half):
        return self.buf.at[kind, sec, pl.ds(pl.multiple_of(half * H, H), H)]

    def copy(self, kind, sec, half, slot, to, index):
        return pltpu.make_async_remote_copy(
            src_ref=self.view(kind, sec, half), dst_ref=self.view(kind, sec, half),
            send_sem=self.send.at[index], recv_sem=self.recv.at[slot], device_id=to, device_id_type=MESH)

    def push(self, kind, sec, half, slot, to):
        c = self.copy(kind, sec, half, slot, to, self.next)
        c.start()
        self.pending.append(c)
        self.next += 1

    def arrived(self, kind, sec, half, slot, to):
        self.copy(kind, sec, half, slot, to, 0).wait_recv()

    def drain(self):
        for c in self.pending:
            c.wait_send()


def spread(buf, send, recv, after=lambda *a: None):
    me, p, x, y_lo, z, core, deep = place()
    dp = lax.axis_index("dp")
    sgn = 2 * y_lo - 1
    row = lambda d: lax.rem(p + d + 4, 4)
    col = lambda d: lax.rem(x + d + 4, 4)
    other_y = dp + (1 - 2 * y_lo) * (2 * deep)
    right, left = (p * 4 + col(1), dp), (p * 4 + col(-1), dp)
    cross = (row(sgn) * 4 + x, other_y)
    pair = (me, other_y)
    sib = (me, dp + 1 - 2 * core)
    greet([right, left, cross, pair, sib])
    SIB = 32

    def run(kind):
        un = Units(buf, send, recv)
        push, got = un.push, un.arrived
        n_sib = [0]

        def share(sec, half):
            push(kind, sec, half, SIB + n_sib[0], sib)
            n_sib[0] += 1

        def x1(r, base):
            sec = r * 4 + x
            push(kind, sec, 0, base + 0, right)
            push(kind, sec, 1, base + 3, left)
            push(kind, sec, 1, base + 1, right)
            push(kind, sec, 0, base + 2, left)

        def y1(t, half, base):
            push(kind, p * 4 + t, half, base + half, cross)

        def x_wait(r, base, which, then=None):
            d, half, who = [(-1, 0, right), (-1, 1, right), (1, 0, left), (1, 1, left), (2, 0, right), (2, 1, left)][which]
            sec = r * 4 + col(d)
            got(kind, sec, half, base + which, who)
            if which == 0:
                push(kind, sec, 0, base + 4, right)
            if which == 3:
                push(kind, sec, 1, base + 5, left)
            if then is not None:
                then(col(d), half)
            share(sec, half)
            after(kind, sec, half)

        def y_wait(t, base, which, then=None):
            if which < 2:
                sec, half, who = row(sgn) * 4 + t, which, cross
            elif which < 4:
                sec, half, who = row(-sgn) * 4 + t, which - 2, pair
            elif which == 4:
                sec, half, who = row(2) * 4 + t, 1 - y_lo, cross
            else:
                sec, half, who = row(2) * 4 + t, y_lo, pair
            got(kind, sec, half, base + which, who)
            if which < 2:
                push(kind, sec, half, base + 2 + which, pair)
            if which == 3:
                push(kind, sec, y_lo, base + 4, cross)
            if which == 4:
                push(kind, sec, half, base + 5, pair)
            if then is not None:
                then(sec // 4, half)
            share(sec, half)
            after(kind, sec, half)

        return un, share, x1, y1, x_wait, y_wait

    def core0():
        un, share, x1, y1, x_wait, y_wait = run(0)
        B = [6, 12, 18, 24]
        x1(p, 0)
        y1(x, 0, B[0]); y1(x, 1, B[0])
        share(me, 0); share(me, 1)
        x_wait(p, 0, 0, lambda t, h: y1(t, h, B[1]))
        x_wait(p, 0, 3, lambda t, h: y1(t, h, B[2]))
        x_wait(p, 0, 1, lambda t, h: y1(t, h, B[1]))
        x_wait(p, 0, 2, lambda t, h: y1(t, h, B[2]))
        y_wait(x, B[0], 0)
        y_wait(x, B[0], 1)
        x_wait(p, 0, 4, lambda t, h: y1(t, h, B[3]))
        x_wait(p, 0, 5, lambda t, h: y1(t, h, B[3]))
        y_wait(x, B[0], 2)
        y_wait(x, B[0], 3)
        ts = [x, col(-1), col(1), col(2)]
        for i in (1, 2, 3):
            for w in (0, 1, 2, 3):
                y_wait(ts[i], B[i], w)
        for i in range(4):
            y_wait(ts[i], B[i], 4)
        for i in range(4):
            y_wait(ts[i], B[i], 5)
        un.drain()

    def core1():
        un, share, x1, y1, x_wait, y_wait = run(1)
        B = [6, 12, 18, 24]
        y1(x, 0, 0); y1(x, 1, 0)
        x1(p, B[0])
        share(me, 0); share(me, 1)
        y_wait(x, 0, 0)
        y_wait(x, 0, 1)
        x1(row(sgn), B[1])
        x_wait(p, B[0], 0)
        x_wait(p, B[0], 3)
        y_wait(x, 0, 2)
        y_wait(x, 0, 3)
        x1(row(-sgn), B[2])
        x_wait(p, B[0], 1)
        x_wait(p, B[0], 2)
        y_wait(x, 0, 4)
        y_wait(x, 0, 5)
        x1(row(2), B[3])
        x_wait(p, B[0], 4)
        x_wait(p, B[0], 5)
        for i, r in ((1, row(sgn)), (2, row(-sgn)), (3, row(2))):
            for w in (0, 3, 1, 2):
                x_wait(r, B[i], w)
        for i, r in ((1, row(sgn)), (2, row(-sgn)), (3, row(2))):
            for w in (4, 5):
                x_wait(r, B[i], w)
        un.drain()

    pl.when(core == 0)(core0)
    pl.when(core == 1)(core1)
    def take(kind, secs):
        un = Units(buf, send, recv)
        for i, (sec, half) in enumerate(secs):
            un.arrived(kind, sec, half, SIB + i, sib)
            after(kind, sec, half)

    far = row(2)
    def order0():
        ts = [x, col(-1), col(1), col(2)]
        o = [(me, 0), (me, 1), (p * 4 + col(-1), 0), (p * 4 + col(1), 1), (p * 4 + col(-1), 1), (p * 4 + col(1), 0)]
        a, b = row(sgn), row(-sgn)
        o += [(a * 4 + x, 0), (a * 4 + x, 1), (p * 4 + col(2), 0), (p * 4 + col(2), 1), (b * 4 + x, 0), (b * 4 + x, 1)]
        for i in (1, 2, 3):
            o += [(a * 4 + ts[i], 0), (a * 4 + ts[i], 1), (b * 4 + ts[i], 0), (b * 4 + ts[i], 1)]
        o += [(far * 4 + t, 1 - y_lo) for t in ts] + [(far * 4 + t, y_lo) for t in ts]
        return o

    def order1():
        a, b = row(sgn), row(-sgn)
        k = lambda r, w: [(r * 4 + col(-1), 0), (r * 4 + col(-1), 1), (r * 4 + col(1), 0), (r * 4 + col(1), 1), (r * 4 + col(2), 0), (r * 4 + col(2), 1)][w]
        o = [(me, 0), (me, 1), (a * 4 + x, 0), (a * 4 + x, 1), k(p, 0), k(p, 3), (b * 4 + x, 0), (b * 4 + x, 1), k(p, 1), k(p, 2),
             (far * 4 + x, 1 - y_lo), (far * 4 + x, y_lo), k(p, 4), k(p, 5)]
        for r in (a, b, far):
            o += [k(r, w) for w in (0, 3, 1, 2)]
        for r in (a, b, far):
            o += [k(r, w) for w in (4, 5)]
        return o

    pl.when(core == 1)(lambda: take(0, order0()))
    pl.when(core == 0)(lambda: take(1, order1()))


def gather_kernel(own_ref, all_ref, send, recv, local):
    me, core = lax.axis_index("section"), lax.rem(lax.axis_index("dp"), 2)
    for kind in range(2):
        c = pltpu.make_async_copy(own_ref.at[kind], all_ref.at[kind, me], local.at[kind])
        pl.when(core == kind)(c.start)
        pl.when(core == kind)(c.wait)
    spread(all_ref, send, recv)


def gather(own, collective_id=1):
    return pl.pallas_call(
        gather_kernel,
        out_shape=jax.ShapeDtypeStruct((2, S) + own.shape[1:], BF16),
        in_specs=[pl.BlockSpec(memory_space=pl.ANY)],
        out_specs=pl.BlockSpec(memory_space=pl.ANY),
        scratch_shapes=[pltpu.SemaphoreType.DMA((64,)), pltpu.SemaphoreType.DMA((64,)), pltpu.SemaphoreType.DMA((2,))],
        compiler_params=pltpu.CompilerParams(collective_id=collective_id, has_side_effects=True),
    )(own)


def swap_kernel(msg_ref, sc_ref, msg_out, sc_out, send, recv, local):
    me, dp = lax.axis_index("section"), lax.axis_index("dp")
    ids = [lax.rem(me + d, S) for d in range(1, S)]
    greet([(i, dp) for i in ids])
    own = [pltpu.make_async_copy(msg_ref.at[me], msg_out.at[me], local.at[0]), pltpu.make_async_copy(sc_ref.at[me], sc_out.at[me], local.at[1])]
    out = []
    for d, i in enumerate(ids):
        for k, (a, b) in enumerate(((msg_ref, msg_out), (sc_ref, sc_out))):
            out.append(pltpu.make_async_remote_copy(
                src_ref=a.at[i], dst_ref=b.at[me], send_sem=send.at[k, d], recv_sem=recv.at[k, d], device_id=(i, dp), device_id_type=MESH))
    for c in out + own:
        c.start()
    for c in out + own:
        c.wait()


def swap(msg, sc, collective_id=2):
    return pl.pallas_call(
        swap_kernel,
        out_shape=(jax.ShapeDtypeStruct(msg.shape, msg.dtype), jax.ShapeDtypeStruct(sc.shape, sc.dtype)),
        in_specs=[pl.BlockSpec(memory_space=pltpu.VMEM)] * 2,
        out_specs=(pl.BlockSpec(memory_space=pltpu.VMEM),) * 2,
        scratch_shapes=[pltpu.SemaphoreType.DMA((2, S)), pltpu.SemaphoreType.DMA((2, S)), pltpu.SemaphoreType.DMA((2,))],
        compiler_params=pltpu.CompilerParams(collective_id=collective_id, has_side_effects=True),
    )(msg, sc)


def reduce_kernel(g_ref, out_ref, near, part, pieces, total, send, recv):
    me, p, x, y_lo, z, core, deep = place()
    dp = lax.axis_index("dp")
    n = 2 * deep
    sib = (me, dp + 1 - 2 * core)
    mine = y_lo * deep + z
    spots = [lax.rem(mine + d, n) for d in range(1, n)]
    ids = [(me, q * 2 + core) for q in spots]
    greet([sib] + ids)
    theirs = 1 - core
    c = pltpu.make_async_remote_copy(
        src_ref=g_ref.at[:, pl.ds(pl.multiple_of(theirs * R, R), R)], dst_ref=near,
        send_sem=send.at[0], recv_sem=recv.at[0], device_id=sib, device_id_type=MESH)
    c.start()
    c.wait()
    for i in range(deep):
        part[i] = (near[i].astype(F32) + g_ref[i, pl.ds(pl.multiple_of(core * R, R), R)].astype(F32)).astype(BF16)

    def piece(q):
        return part.at[lax.rem(q, deep), pl.ds(pl.multiple_of((q // deep) * H, H), H)]
    out = []
    for d, q in enumerate(spots):
        out.append(pltpu.make_async_remote_copy(
            src_ref=piece(q), dst_ref=pieces.at[d], send_sem=send.at[1 + d], recv_sem=recv.at[1 + d], device_id=ids[d], device_id_type=MESH))
        out[-1].start()
    acc = piece(mine)[...].astype(F32)
    for d, cpy in enumerate(out):
        cpy.wait_recv()
        acc = acc + pieces[d].astype(F32)
    total[...] = acc.astype(BF16)
    back = []
    for d, q in enumerate(spots):
        back.append(pltpu.make_async_remote_copy(
            src_ref=total, dst_ref=out_ref.at[core, mine], send_sem=send.at[n + d], recv_sem=recv.at[n + d], device_id=ids[d], device_id_type=MESH))
        back[-1].start()
    out_ref[core, mine] = total[...]
    hand = []

    def share(kind, spot, slot):
        return pltpu.make_async_remote_copy(
            src_ref=out_ref.at[kind, spot], dst_ref=out_ref.at[kind, spot], send_sem=send.at[2 * n + slot], recv_sem=recv.at[2 * n + slot],
            device_id=sib, device_id_type=MESH)
    hand.append(share(core, mine, 0))
    hand[-1].start()
    for d in range(n - 1):
        src = lax.rem(mine + n - 1 - d, n)
        pltpu.make_async_remote_copy(
            src_ref=total, dst_ref=out_ref.at[core, src], send_sem=send.at[n + d], recv_sem=recv.at[n + d], device_id=ids[d], device_id_type=MESH).wait_recv()
        hand.append(share(core, src, 1 + d))
        hand[-1].start()
    for d in range(n):
        src = lax.rem(mine + n - d, n)
        share(theirs, src, d).wait_recv()
    for cpy in out + back + hand:
        cpy.wait_send()


def reduce(g, collective_id=3):
    deep, _, cols = g.shape
    n = 2 * deep
    return pl.pallas_call(
        reduce_kernel,
        out_shape=jax.ShapeDtypeStruct((2, n, H, cols), BF16),
        in_specs=[pl.BlockSpec(memory_space=pltpu.VMEM)],
        out_specs=pl.BlockSpec(memory_space=pltpu.VMEM),
        scratch_shapes=[
            pltpu.VMEM((deep, R, cols), BF16), pltpu.VMEM((deep, R, cols), BF16), pltpu.VMEM((n, H, cols), BF16), pltpu.VMEM((H, cols), BF16),
            pltpu.SemaphoreType.DMA((3 * n + 1,)), pltpu.SemaphoreType.DMA((3 * n + 1,))],
        compiler_params=pltpu.CompilerParams(collective_id=collective_id, has_side_effects=True, vmem_limit_bytes=40 * 2**20),
    )(g)


def on_device(x_down, x_up, cot_down, cot_up, gain, w_a, w_b):
    width = x_down.shape[-1]
    me = lax.axis_index("section")
    rows = MBS * 8
    xd, xu, cd, cu = [t.reshape(rows, width) for t in (x_down, x_up, cot_down, cot_up)]
    gf, wa = gain[0].astype(F32), w_a[0].astype(F32)
    own = jnp.stack([(gf * wa).astype(BF16), w_b[0]])
    w = gather(own).reshape(2 * LANES, width)

    def mine(down, up):
        at = lax.rem(me, MBS) * 8
        return jnp.where(me < MBS, lax.dynamic_slice_in_dim(down, at, 8), lax.dynamic_slice_in_dim(up, at, 8))

    picked = jnp.concatenate([mine(xd, xu), mine(cd, cu)], axis=0)
    msg, sc = swap(*chain(picked, w))
    partial = final(msg, sc, xd, xu, cd, cu, w)
    total = reduce(partial)
    deep, cols = partial.shape[0], partial.shape[2]
    total = total.reshape(2, 2, deep, H, cols).transpose(0, 1, 3, 2, 4).reshape(2, R, width).astype(F32)
    return ((wa * total[0]).sum(0)[None], (gf * total[0])[None], total[1][None])


def solution(mesh):
    data, held = P("dp", None, None, None), P("section", None, None)
    return jax.shard_map(
        on_device,
        mesh=mesh,
        in_specs=(data, data, data, data, P("section", None), held, held),
        out_specs=(P("section", None), held, held),
        check_vma=False,
    )
```

```python
import jax
import jax.numpy as jnp
from jax import lax
from jax.experimental import pallas as pl
from jax.experimental.pallas import tpu as pltpu
from jax.sharding import PartitionSpec as P

F32, BF16 = jnp.float32, jnp.bfloat16
S, R, H = 16, 32, 16
ALL = S * R
ROWS = 128
MESH = pl.DeviceIdType.MESH
NT = (((1,), (1,)), ((), ()))
NN = (((1,), (0,)), ((), ()))

FIRST_A = (
    (0, "xl", 1), (0, "y1", 0, 0), (0, "xr", 0), (0, "xr", 1), (0, "y1", 0, 1), (0, "xl", 0),
)
ORDER_A = (
    (0, "y1", 0, 0), (0, "xl", 1), (0, "xr", 0), (0, "xl", 0), (0, "y1", 0, 1), (0, "x2r"),
    (0, "y1", 2, 1), (0, "y1", 1, 0), (0, "xr", 1), (0, "y1", 2, 0), (0, "y2", 0, 1), (0, "y2", 2, 1),
    (0, "y2", 0, 0), (0, "x2l"), (0, "y2", 1, 0), (0, "y1", 3, 0), (0, "y1", 1, 1), (0, "y3", 0),
    (0, "y2", 2, 0), (0, "y1", 3, 1), (0, "y2", 3, 0), (0, "y3", 1), (0, "y3", 2), (0, "y4", 0),
    (0, "y3", 3), (0, "y4", 1), (0, "y4", 3), (0, "y2", 1, 1), (0, "y4", 2), (0, "y2", 3, 1),
)
FIRST_B = (
    (1, "xr", 0, 1), (1, "xl", 0, 0), (1, "y1", 0), (1, "xl", 0, 1), (1, "y1", 1), (1, "xr", 0, 0),
)
ORDER_B = (
    (1, "y1", 0), (1, "y1", 1), (1, "xl", 0, 1), (1, "y2", 0), (1, "xr", 0, 0), (1, "xr", 1, 1),
    (1, "y2", 1), (1, "xr", 1, 0), (1, "xr", 0, 1), (1, "xl", 1, 1), (1, "y3"), (1, "xl", 2, 0),
    (1, "xl", 2, 1), (1, "xr", 2, 0), (1, "x2r", 0), (1, "y4"), (1, "xl", 3, 1), (1, "xr", 2, 1),
    (1, "x2l", 2), (1, "xl", 0, 0), (1, "x2r", 1), (1, "xl", 3, 0), (1, "x2r", 2), (1, "xl", 1, 0),
    (1, "xr", 3, 0), (1, "xr", 3, 1), (1, "x2l", 0), (1, "x2r", 3), (1, "x2l", 1), (1, "x2l", 3),
)


def dot(a, b, dims=NN):
    return lax.dot_general(a, b, dims, preferred_element_type=F32)


def gelu_pair(h):
    k = 0.7978845608028654
    t = jnp.tanh(k * (h + 0.044715 * h * h * h))
    up = 0.5 * (1.0 + t)
    return h * up, up + 0.5 * h * (1.0 - t * t) * (k * (1.0 + 3 * 0.044715 * h * h))


def halves(m):
    hi = m.astype(BF16)
    return hi, (m - hi.astype(F32)).astype(BF16)


class Place:
    def __init__(self):
        self.me, self.dp = lax.axis_index("section"), lax.axis_index("dp")
        self.deep = lax.axis_size("dp") // 4
        self.p, self.x = self.me // 4, lax.rem(self.me, 4)
        self.core = lax.rem(self.dp, 2)
        self.z = lax.rem(self.dp // 2, self.deep)
        self.y_lo = self.dp // (2 * self.deep)
        self.sgn = 2 * self.y_lo - 1
        other = self.dp + (1 - 2 * self.y_lo) * (2 * self.deep)
        self.right, self.left = (self.p * 4 + self.col(1), self.dp), (self.p * 4 + self.col(-1), self.dp)
        self.cross, self.pair = (self.row(self.sgn) * 4 + self.x, other), (self.me, other)
        self.sib = (self.me, self.dp + 1 - 2 * self.core)

    def row(self, d):
        return lax.rem(self.p + d + 4, 4)

    def col(self, d):
        return lax.rem(self.x + d + 4, 4)

    def spot(self, d, e):
        y = self.y_lo if e == 0 else 1 - self.y_lo
        z = lax.rem(self.z + d + self.deep, self.deep)
        return y, z, (self.me, (y * self.deep + z) * 2 + self.core)


def greet(partners):
    barrier = pltpu.get_barrier_semaphore()
    for partner in partners:
        pl.semaphore_signal(barrier, inc=1, device_id=partner, device_id_type=MESH)
    pl.semaphore_wait(barrier, len(partners))


def remote(src, dst, send, recv, to):
    return pltpu.make_async_remote_copy(src_ref=src, dst_ref=dst, send_sem=send, recv_sem=recv, device_id=to, device_id_type=MESH)


def route(at, name):
    me, p, x, y = at.me, at.p, at.x, at.y_lo
    hy = lambda h: y if h == 0 else 1 - y
    hn = lambda h: 1 - y if h == 0 else y
    near, away, far = at.row(at.sgn), at.row(-at.sgn), at.row(2)
    lft, rgt, opp = at.col(-1), at.col(1), at.col(2)
    kind, what, rest = name[0], name[1], name[2:]
    if kind == 0:
        if what in ("xr", "xl"):
            h = hy(rest[0])
            return (me, h), at.right if what == "xr" else at.left, (p * 4 + (lft if what == "xr" else rgt), h)
        if what == "x2r":
            return (p * 4 + lft, hy(0)), at.right, (p * 4 + opp, hy(0))
        if what == "x2l":
            return (p * 4 + rgt, hy(1)), at.left, (p * 4 + opp, hy(1))
        t = (x, lft, rgt, opp)[rest[0]]
        base, rest = p * 4 + t, rest[1:]
    else:
        if what in ("xr", "xl", "x2r", "x2l"):
            r = (p, near, away, far)[rest[0]]
            if what in ("xr", "xl"):
                h = hn(rest[1]) if rest[0] == 1 else hy(rest[1])
                return (r * 4 + x, h), at.right if what == "xr" else at.left, (r * 4 + (lft if what == "xr" else rgt), h)
            k = 0 if what == "x2r" else 1
            h = hn(k) if rest[0] == 1 else hy(k)
            return (r * 4 + (lft if k == 0 else rgt), h), at.right if k == 0 else at.left, (r * 4 + opp, h)
        t, base = x, me
    if what == "y1":
        return (base, hy(rest[0])), at.cross, (near * 4 + t, hn(rest[0]))
    if what == "y2":
        return (near * 4 + t, hn(rest[0])), at.pair, (away * 4 + t, hy(rest[0]))
    if what == "y3":
        return (away * 4 + t, y), at.cross, (far * 4 + t, 1 - y)
    return (far * 4 + t, 1 - y), at.pair, (far * 4 + t, y)


def needs(name):
    kind, what, rest = name[0], name[1], name[2:]
    if kind == 0:
        if what in ("xr", "xl"):
            return None
        if what == "x2r":
            return (0, "xr", 0)
        if what == "x2l":
            return (0, "xl", 1)
        t = rest[0]
        if what == "y1":
            return (None, (0, "xr", rest[1]), (0, "xl", rest[1]), (0, "x2r") if rest[1] == 0 else (0, "x2l"))[t]
        return {"y2": (0, "y1", t) + rest[1:], "y3": (0, "y2", t, 0), "y4": (0, "y3", t)}[what]
    if what == "y1":
        return None
    if what in ("y2", "y3", "y4"):
        return {"y2": (1, "y1") + rest, "y3": (1, "y2", 0), "y4": (1, "y3")}[what]
    if what in ("xr", "xl"):
        return (None, (1, "y1", rest[1]), (1, "y2", rest[1]), (1, "y4") if rest[1] == 0 else (1, "y3"))[rest[0]]
    return (1, "xr", rest[0], 0) if what == "x2r" else (1, "xl", rest[0], 1)


def spread(at, w, send, recv, prepare):
    def view(kind, unit):
        return w.at[kind, unit[0], pl.ds(pl.multiple_of(unit[1] * H, H), H)]

    def run(kind, first, order):
        slot = {name: i for i, name in enumerate(order)}
        sent = []

        def push(name):
            unit, to, _ = route(at, name)
            c = remote(view(kind, unit), view(kind, unit), send.at[slot[name]], recv.at[slot[name]], to)
            c.start()
            sent.append(c)

        for name in first:
            push(name)
        prepare()
        for i, name in enumerate(order):
            unit, to = route(at, name)[2], route(at, name)[1]
            got = view(kind, unit)
            remote(got, got, send.at[i], recv.at[i], to).wait_recv()
            for later in order:
                if needs(later) == name:
                    push(later)
            c = remote(got, got, send.at[32 + i], recv.at[32 + i], at.sib)
            c.start()
            sent.append(c)
        for c in sent:
            c.wait_send()

    def take(kind, order):
        for i, name in enumerate(order):
            got = view(kind, route(at, name)[2])
            remote(got, got, send.at[32 + i], recv.at[32 + i], at.sib).wait_recv()

    pl.when(at.core == 0)(lambda: run(0, FIRST_A, ORDER_A))
    pl.when(at.core == 1)(lambda: run(1, FIRST_B, ORDER_B))
    pl.when(at.core == 1)(lambda: take(0, ORDER_A))
    pl.when(at.core == 0)(lambda: take(1, ORDER_B))


def grams(w, rows, raw, gg, mm):
    width = rows.shape[1]

    def block(i, _):
        lhs = w[i // 2, pl.ds(lax.rem(i, 2) * 8, 8)].reshape(256, width)
        for b in range(2):
            raw[i, :, b * 256:(b + 1) * 256] = dot(lhs, w[1, b * 8:(b + 1) * 8].reshape(256, width), NT)
        raw[i, :, 512:768] = dot(lhs, rows[...], NT)
        raw[i, :, 768:896] = dot(lhs, jnp.ones((ROWS, width), BF16), NT)
        return 0

    lax.fori_loop(0, 4, block, 0)
    for i in range(4):
        for g in range(4):
            hi, lo = halves(raw[i, :, g * 128:(g + 1) * 128])
            gg[g, i * 256:(i + 1) * 256, 0:128] = hi
            gg[g, i * 256:(i + 1) * 256, 128:256] = lo
    for j in range(4):
        for s in range(j + 1):
            hi, lo = halves(raw[j // 2, (j % 2) * 128:(j % 2 + 1) * 128, s * 128:(s + 1) * 128].T)
            mm[j, s * 128:(s + 1) * 128, 0:128] = hi
            mm[j, s * 128:(s + 1) * 128, 128:256] = lo


def chain(width, stat, raw, gg, mm, u, v, c, acts, ds, fs, sc):
    for i in range(2):
        half = slice(i * 256, (i + 1) * 256)
        u[half] = raw[i, :, 640:768]
        v[half] = raw[2 + i, :, 640:768]
        c[half] = raw[2 + i, :, 512:640]

    def sums(kind, s):
        return raw[kind * 2 + s // 8, (s % 8) * R:(s % 8 + 1) * R, 768:896]

    def spot(a, s):
        o = s % 4
        parts = [jnp.zeros((o * R, ROWS), BF16)] * (o > 0) + [a] + [jnp.zeros(((3 - o) * R, ROWS), BF16)] * (o < 3)
        padded = jnp.concatenate(parts, axis=0) if len(parts) > 1 else a
        return jnp.concatenate([padded, padded], axis=0)

    total = lambda t: jnp.sum(t, axis=0, keepdims=True)
    mu, q = stat[0:1], stat[1:2]
    hid, slope, rstds, mus, kept, held = [], [], [], [], [], []
    for s in range(S):
        sl = slice(s * R, (s + 1) * R)
        rstd = lax.rsqrt(q * (1.0 / width) + 1e-5)
        h = rstd * (u[sl] - mu * sums(0, s))
        a, g = gelu_pair(h)
        a16 = a.astype(BF16)
        af = a16.astype(F32)
        acts[s] = a16
        old = v[sl]
        hid.append(h)
        slope.append(g)
        rstds.append(rstd)
        mus.append(mu)
        kept.append(old)
        held.append(af)
        if s < S - 1:
            rhs = spot(a16, s)
            wbs = sums(1, s)
            u[(s + 1) * R:] += dot(gg[s // 4, (s + 1) * R:ALL], rhs)
            new_v = v[s * R:] + dot(gg[s // 4, ALL + s * R:], rhs)
            v[s * R:] = new_v
            tot = total(af * wbs)
            q = q + total(af * (old + new_v[0:R] - (2.0 * mu) * wbs)) - tot * tot * (1.0 / width)
            q = jnp.maximum(q, 0.0)
            mu = mu + tot * (1.0 / width)
    cc, ee = jnp.zeros_like(mu), jnp.zeros_like(mu)
    blank = jnp.zeros((5, ROWS), F32)
    ds[S - 1] = jnp.zeros((R, ROWS), BF16)
    for j in range(S - 1, -1, -1):
        sl = slice(j * R, (j + 1) * R)
        sc[j] = jnp.concatenate([mus[j], cc, ee, blank], axis=0)
        da = c[sl] - cc * kept[j] - ee * sums(1, j)
        f16 = (rstds[j] * (da * slope[j])).astype(BF16)
        fs[j] = f16
        f = f16.astype(F32)
        a_j = total(f * sums(0, j)) * (1.0 / width)
        c_j = rstds[j] * total(f * hid[j]) * (1.0 / width)
        cc = cc + c_j
        ee = ee + a_j - c_j * mus[j]
        if j > 0:
            d16 = (held[j - 1] * cc).astype(BF16)
            ds[j - 1] = d16
            c[0:j * R] += dot(mm[j // 4, 0:j * R], spot(f16, j)) - dot(gg[(j - 1) // 4, ALL:ALL + j * R], spot(d16, j - 1))


def kernel(xd, xu, cd, cu, gain, wa, wb, gg_out, ga_out, gb_out,
           w, rows, stat, raw, gg, mm, u, v, c, acts, ds, fs, sc, half, near, part, pieces, total, tot,
           send, recv, rs_send, rs_recv, a2a_send, a2a_recv, ag_send, ag_recv, sh_send, sh_recv):
    at = Place()
    me, core, deep = at.me, at.core, at.deep
    width = rows.shape[1]
    step = width // deep
    far_first = sorted(range(deep), key=lambda d: (-min(d, deep - d), d))
    spots = [(k, e) for k in range(deep) for e in range(2) if (far_first[k], e) != (0, 0)]
    w[0, me] = (gain[...].astype(F32) * wa[...].astype(F32)).astype(BF16)
    w[1, me] = wb[...]
    greet([at.right, at.left, at.cross, at.sib] + [at.spot(far_first[k], e)[2] for k, e in spots])

    def prepare():
        for i, ref in enumerate((cd, cu, xd, xu)):
            for b in range(4):
                val = jnp.concatenate([ref[2 * b].astype(F32), ref[2 * b + 1].astype(F32)], axis=0)
                rows[i * 64 + b * 16:i * 64 + (b + 1) * 16] = val.astype(BF16)
        mus, qs = [], []
        for ref in (xd, xu):
            for b in range(8):
                val = ref[b].astype(F32)
                mean = jnp.sum(val, axis=1, keepdims=True) * (1.0 / width)
                val = val - mean
                mus.append(mean)
                qs.append(jnp.sum(val * val, axis=1, keepdims=True))
        wide = lambda t: jnp.broadcast_to(jnp.concatenate(t, axis=0), (ROWS, ROWS)).T[0:1]
        stat[0:1] = wide(mus)
        stat[1:2] = wide(qs)

    spread(at, w, send, recv, prepare)
    grams(w, rows, raw, gg, mm)
    chain(width, stat, raw, gg, mm, u, v, c, acts, ds, fs, sc)

    at_row = lax.broadcasted_iota(jnp.int32, (ALL, ROWS), 0)
    flat = lambda ref: ref[...].reshape(ALL, ROWS).astype(F32)
    turn = lambda t: t.T.astype(BF16)
    zx = turn(jnp.where(at_row < me * R, flat(acts), 0.0))
    zd = turn(jnp.where(at_row >= me * R, flat(ds), 0.0))
    fd = turn(jnp.where(at_row >= (me + 1) * R, flat(fs), 0.0))
    zxd = jnp.concatenate([zx, zd], axis=0)
    own = jnp.concatenate([sc[me], jnp.zeros((ROWS - 8, ROWS), F32)], axis=0).T
    mu, cc, ee = own[:, 0:1], own[:, 1:2], own[:, 2:3]
    act, f = acts[me], fs[me]

    def block(k):
        z = at.spot(far_first[k], 0)[1]
        cols = pl.ds(pl.multiple_of(z * step, step), step)
        from_b = dot(zxd, w[1, :, :, cols].reshape(ALL, step))
        x = rows[ROWS:, cols].astype(F32) + from_b[0:ROWS]
        dy = rows[0:ROWS, cols].astype(F32) + dot(fd, w[0, :, :, cols].reshape(ALL, step)) - from_b[ROWS:] - cc * x - ee
        half[k, 0:R] = dot(f, (x - mu).astype(BF16)).astype(BF16)
        half[k, R:] = dot(act, dy.astype(BF16)).astype(BF16)
        out = remote(half.at[k, pl.ds(pl.multiple_of((1 - core) * R, R), R)], near.at[k], rs_send.at[k], rs_recv.at[k], at.sib)
        out.start()
        return out

    def piece(k, e):
        y = at.y_lo if e == 0 else 1 - at.y_lo
        return part.at[k, pl.ds(pl.multiple_of(y * H, H), H)]

    out, moved = [], []
    for k in range(deep + 1):
        if k < deep:
            out.append(block(k))
        if k > 0:
            b = k - 1
            out[b].wait_recv()
            part[b] = (near[b].astype(F32) + half[b, pl.ds(pl.multiple_of(core * R, R), R)].astype(F32)).astype(BF16)
            for e in range(2):
                if (b, e) in spots:
                    n = 2 * b + e
                    moved.append(remote(piece(b, e), pieces.at[n], a2a_send.at[n], a2a_recv.at[n], at.spot(far_first[b], e)[2]))
                    moved[-1].start()
    acc = piece(far_first.index(0), 0)[...].astype(F32)
    for copy, (k, e) in zip(moved, spots):
        copy.wait_recv()
        acc = acc + pieces[2 * k + e].astype(F32)
    total[...] = acc.astype(BF16)

    def landing(kind, y, z):
        return tot.at[kind, pl.ds(pl.multiple_of(y * H, H), H), pl.ds(pl.multiple_of(z * step, step), step)]

    mine = landing(core, at.y_lo, at.z)
    for k, e in spots:
        n = 2 * k + e
        moved.append(remote(total, mine, ag_send.at[n], ag_recv.at[n], at.spot(far_first[k], e)[2]))
        moved[-1].start()
    mine[...] = total[...]
    moved.append(remote(mine, mine, sh_send.at[0], sh_recv.at[0], at.sib))
    moved[-1].start()
    came = [(at.y_lo, at.z)]
    for i, (k, e) in enumerate(spots):
        n = 2 * k + e
        y, z, to = at.spot(-far_first[k], e)
        got = landing(core, y, z)
        came.append((y, z))
        remote(got, got, ag_send.at[n], ag_recv.at[n], to).wait_recv()
        moved.append(remote(got, got, sh_send.at[1 + i], sh_recv.at[1 + i], at.sib))
        moved[-1].start()
    for i, (y, z) in enumerate(came):
        got = landing(1 - core, y, z)
        remote(got, got, sh_send.at[i], sh_recv.at[i], at.sib).wait_recv()
    for i in range(deep):
        cols = slice(i * step, (i + 1) * step)
        h = tot[0, :, cols].astype(F32)
        ga_out[:, cols] = gain[:, cols].astype(F32) * h
        gg_out[:, cols] = jnp.sum(wa[:, cols].astype(F32) * h, axis=0, keepdims=True)
        gb_out[:, cols] = tot[1, :, cols].astype(F32)
    for copy in out + moved:
        copy.wait_send()


def on_device(x_down, x_up, cot_down, cot_up, gain, w_a, w_b):
    width = x_down.shape[-1]
    deep = lax.axis_size("dp") // 4
    step = width // deep
    vmem = pl.BlockSpec(memory_space=pltpu.VMEM)
    sems = lambda n: [pltpu.SemaphoreType.DMA((n,)), pltpu.SemaphoreType.DMA((n,))]
    gg, ga, gb = pl.pallas_call(
        kernel,
        out_shape=(
            jax.ShapeDtypeStruct((1, width), F32),
            jax.ShapeDtypeStruct((R, width), F32),
            jax.ShapeDtypeStruct((R, width), F32),
        ),
        in_specs=[vmem] * 7,
        out_specs=(vmem,) * 3,
        scratch_shapes=[
            pltpu.VMEM((2, S, R, width), BF16),
            pltpu.VMEM((2 * ROWS, width), BF16),
            pltpu.VMEM((8, ROWS), F32),
            pltpu.VMEM((4, 256, 896), F32),
            pltpu.VMEM((4, 2 * ALL, 256), BF16),
            pltpu.VMEM((4, ALL, 256), BF16),
            pltpu.VMEM((ALL, ROWS), F32),
            pltpu.VMEM((ALL, ROWS), F32),
            pltpu.VMEM((ALL, ROWS), F32),
            pltpu.VMEM((S, R, ROWS), BF16),
            pltpu.VMEM((S, R, ROWS), BF16),
            pltpu.VMEM((S, R, ROWS), BF16),
            pltpu.VMEM((S, 8, ROWS), F32),
            pltpu.VMEM((deep, 2 * R, step), BF16),
            pltpu.VMEM((deep, R, step), BF16),
            pltpu.VMEM((deep, R, step), BF16),
            pltpu.VMEM((2 * deep, H, step), BF16),
            pltpu.VMEM((H, step), BF16),
            pltpu.VMEM((2, R, width), BF16),
        ]
        + sems(64) + sems(deep) + sems(2 * deep) + sems(2 * deep) + sems(2 * deep),
        compiler_params=pltpu.CompilerParams(collective_id=0, has_side_effects=True, vmem_limit_bytes=56 * 2**20),
    )(x_down[0], x_up[0], cot_down[0], cot_up[0], gain, w_a[0], w_b[0])
    return gg, ga[None], gb[None]


def solution(mesh):
    data, held = P("dp", None, None, None), P("section", None, None)
    return jax.shard_map(
        on_device,
        mesh=mesh,
        in_specs=(data, data, data, data, P("section", None), held, held),
        out_specs=(P("section", None), held, held),
        check_vma=False,
    )
```

```python
import jax
import jax.numpy as jnp
from jax import lax
from jax.experimental import pallas as pl
from jax.experimental.pallas import tpu as pltpu
from jax.sharding import PartitionSpec as P

F32, BF16 = jnp.float32, jnp.bfloat16
S, R, H = 16, 32, 16
ALL = S * R
ROWS = 128
MESH = pl.DeviceIdType.MESH
NT = (((1,), (1,)), ((), ()))
NN = (((1,), (0,)), ((), ()))

FIRST_A = (
    (0, "xl", 0), (0, "xr", 0), (0, "xr", 1), (0, "y1", 0, 0), (0, "y1", 0, 1), (0, "xl", 1),
)
ORDER_A = (
    (0, "xr", 0), (0, "y1", 0, 0), (0, "xl", 0), (0, "xr", 1), (0, "y1", 0, 1), (0, "xl", 1),
    (0, "x2r", 0), (0, "y1", 1, 0), (0, "x2l", 0), (0, "y1", 2, 0), (0, "x2r", 1), (0, "y1", 1, 1),
    (0, "x2l", 1), (0, "z", 3), (0, "z", 6), (0, "y2", 0, 0), (0, "z", 0), (0, "y1", 2, 1),
    (0, "y2", 1, 0), (0, "y1", 3, 0), (0, "y2", 2, 0), (0, "y2", 0, 1), (0, "y2", 1, 1), (0, "y1", 3, 1),
    (0, "y2", 2, 1), (0, "y3", 1, 0), (0, "y2", 3, 0), (0, "z", 1), (0, "z", 7), (0, "y3", 0, 0),
    (0, "y3", 2, 0), (0, "y3", 1, 1), (0, "z", 12), (0, "y2", 3, 1), (0, "z", 4), (0, "y3", 3, 0),
    (0, "y4", 1, 0), (0, "y4", 0, 0), (0, "y3", 0, 1), (0, "y4", 2, 0), (0, "z", 9), (0, "y3", 2, 1),
    (0, "y4", 1, 1), (0, "y3", 3, 1), (0, "y4", 3, 0), (0, "z", 10), (0, "y4", 0, 1), (0, "z", 11),
    (0, "y4", 2, 1), (0, "z", 8), (0, "z", 5), (0, "y4", 3, 1), (0, "z", 2), (0, "z", 13),
    (0, "z", 14),
)
FIRST_B = (
    (1, "y1", 0), (1, "y1", 1), (1, "xr", 0, 0), (1, "xr", 0, 1), (1, "xl", 0, 0), (1, "xl", 0, 1),
)
ORDER_B = (
    (1, "y1", 0), (1, "xr", 0, 0), (1, "y1", 1), (1, "xl", 0, 0), (1, "xl", 0, 1), (1, "y2", 0),
    (1, "xr", 0, 1), (1, "xl", 1, 1), (1, "xl", 1, 0), (1, "y2", 1), (1, "xr", 1, 1), (1, "y3", 0),
    (1, "xr", 1, 0), (1, "xr", 2, 0), (1, "x2l", 1, 1), (1, "z", 0), (1, "xl", 2, 0), (1, "x2l", 0, 0),
    (1, "x2l", 0, 1), (1, "y3", 1), (1, "x2r", 0, 1), (1, "xr", 2, 1), (1, "z", 4), (1, "y4", 0),
    (1, "x2r", 0, 0), (1, "x2r", 1, 0), (1, "x2l", 2, 0), (1, "x2l", 1, 0), (1, "z", 3), (1, "y4", 1),
    (1, "x2r", 2, 0), (1, "xr", 3, 0), (1, "xl", 3, 0), (1, "xl", 2, 1), (1, "x2r", 1, 1), (1, "z", 5),
    (1, "xr", 3, 1), (1, "x2r", 3, 0), (1, "x2l", 3, 0), (1, "xl", 3, 1), (1, "x2l", 2, 1), (1, "z", 9),
    (1, "z", 13), (1, "z", 10), (1, "z", 2), (1, "x2r", 3, 1), (1, "z", 6), (1, "z", 8),
    (1, "z", 7), (1, "x2r", 2, 1), (1, "z", 12), (1, "z", 14), (1, "z", 11), (1, "x2l", 3, 1),
    (1, "z", 1),
)
BROUGHT = (
    [((0, "xr"),), ((0, "xl"),), ((0, "x2r"), (0, "x2l"))]
    + [b for t in range(4) for b in (((0, "y1", t),), ((0, "y2", t),), ((0, "y3", t), (0, "y4", t)))],
    [((1, "y1"),), ((1, "y2"),), ((1, "y3"), (1, "y4"))]
    + [b for r in range(4) for b in (((1, "xr", r),), ((1, "xl", r),), ((1, "x2r", r), (1, "x2l", r)))],
)


def dot(a, b, dims=NN):
    return lax.dot_general(a, b, dims, preferred_element_type=F32)


def gelu_pair(h):
    k = 0.7978845608028654
    t = jnp.tanh(k * (h + 0.044715 * h * h * h))
    up = 0.5 * (1.0 + t)
    return h * up, up + 0.5 * h * (1.0 - t * t) * (k * (1.0 + 3 * 0.044715 * h * h))


def halves(m):
    hi = m.astype(BF16)
    return hi, (m - hi.astype(F32)).astype(BF16)


class Place:
    def __init__(self):
        self.me, self.dp = lax.axis_index("section"), lax.axis_index("dp")
        self.deep = lax.axis_size("dp") // 4
        self.p, self.x = self.me // 4, lax.rem(self.me, 4)
        self.core = lax.rem(self.dp, 2)
        self.z = lax.rem(self.dp // 2, self.deep)
        self.y_lo = self.dp // (2 * self.deep)
        self.sgn = 2 * self.y_lo - 1
        other = self.dp + (1 - 2 * self.y_lo) * (2 * self.deep)
        self.right, self.left = (self.p * 4 + self.col(1), self.dp), (self.p * 4 + self.col(-1), self.dp)
        self.cross, self.pair = (self.row(self.sgn) * 4 + self.x, other), (self.me, other)
        self.sib = (self.me, self.dp + 1 - 2 * self.core)

    def row(self, d):
        return lax.rem(self.p + d + 4, 4)

    def col(self, d):
        return lax.rem(self.x + d + 4, 4)

    def spot(self, d, e):
        y = self.y_lo if e == 0 else 1 - self.y_lo
        z = lax.rem(self.z + d + self.deep, self.deep)
        return y, z, (self.me, (y * self.deep + z) * 2 + self.core)


def greet(partners):
    barrier = pltpu.get_barrier_semaphore()
    for partner in partners:
        pl.semaphore_signal(barrier, inc=1, device_id=partner, device_id_type=MESH)
    pl.semaphore_wait(barrier, len(partners))


def remote(src, dst, send, recv, to):
    return pltpu.make_async_remote_copy(src_ref=src, dst_ref=dst, send_sem=send, recv_sem=recv, device_id=to, device_id_type=MESH)


def route(at, name):
    p, x, y = at.p, at.x, at.y_lo
    near, away, far = at.row(at.sgn), at.row(-at.sgn), at.row(2)
    lft, rgt, opp = at.col(-1), at.col(1), at.col(2)
    kind, what = name[0], name[1]
    if what[0] == "x":
        r = (p, near, away, far)[name[2] if kind else 0] * 4
        return {
            "xr": ((r + x, None), at.right, (r + lft, None)),
            "xl": ((r + x, None), at.left, (r + rgt, None)),
            "x2r": ((r + lft, y), at.right, (r + opp, y)),
            "x2l": ((r + rgt, 1 - y), at.left, (r + opp, 1 - y)),
        }[what]
    t = x if kind else (x, lft, rgt, opp)[name[2]]
    return {
        "y1": ((p * 4 + t, None), at.cross, (near * 4 + t, None)),
        "y2": ((near * 4 + t, None), at.pair, (away * 4 + t, None)),
        "y3": ((away * 4 + t, y), at.cross, (far * 4 + t, 1 - y)),
        "y4": ((far * 4 + t, 1 - y), at.pair, (far * 4 + t, y)),
    }[what]


def needs(name):
    kind, what, rest, q = name[0], name[1], name[2:-1], name[-1:]
    if what == "z":
        return [base + (0,) for base in BROUGHT[kind][name[2]]]
    if what in ("x2r", "x2l"):
        return [(kind, "xr" if what == "x2r" else "xl") + rest + q]
    if what in ("y2", "y3", "y4"):
        return [(kind, {"y2": "y1", "y3": "y2", "y4": "y3"}[what]) + rest + q]
    if kind == 0 and what == "y1":
        return [[], [(0, "xr") + q], [(0, "xl") + q], [(0, "x2r") + q, (0, "x2l") + q]][rest[0]]
    if kind == 1 and what in ("xr", "xl"):
        return [[], [(1, "y1") + q], [(1, "y2") + q], [(1, "y3") + q, (1, "y4") + q]][rest[0]]
    return []


def sum_tiles(w, kind, sec, first, last):
    acc = w[kind, sec, :, first:first + 128].astype(F32)
    for col in range(first + 128, last, 128):
        acc = acc + w[kind, sec, :, col:col + 128].astype(F32)
    return acc


def spread(at, w, sums, send, recv, prepare):
    width = w.shape[-1]
    part = width // 128 * 3 // 10 * 128
    parity = lax.rem(at.z, 2)
    up, down = at.spot(1, 0)[2], at.spot(-1, 0)[2]

    def view(kind, unit, q):
        rows = pl.ds(0, R) if unit[1] is None else pl.ds(pl.multiple_of(unit[1] * H, H), H)
        cols = pl.ds(2 * part, width - 2 * part) if q else pl.ds(pl.multiple_of(parity * part, 128), part)
        return w.at[kind, unit[0], rows, cols]

    def strip(kind, sec, side, which):
        start = side * part + which * (part // 2)
        return w.at[kind, sec, :, pl.ds(pl.multiple_of(start, 128), part // 2)]

    def handed(kind, sec, q):
        return w.at[kind, sec, :, pl.ds(2 * part, width - 2 * part) if q else pl.ds(0, 2 * part)]

    def tally(kind, sec, q):
        sums[kind, sec] += sum_tiles(w, kind, sec, 2 * part if q else 0, width if q else 2 * part)

    def section(kind, i):
        return route(at, BROUGHT[kind][i][0])[2][0]

    def ends(kind, order):
        found = []
        for n, name in enumerate(order):
            if name[1] == "z":
                found.append((n, name[2], 0))
            elif name[-1] == 1:
                for i, bases in enumerate(BROUGHT[kind]):
                    if name[:-1] in bases and all(order.index(base + (1,)) <= n for base in bases):
                        found.append((n, i, 1))
        return found

    def run(kind, first, order):
        sent, seen = [], set()
        over = {n: (i, q) for n, i, q in ends(kind, order)}

        def start(src, dst, index, to):
            c = remote(src, dst, send.at[index], recv.at[index], to)
            c.start()
            sent.append(c)

        def push(name):
            n = order.index(name)
            if name[1] == "z":
                for which, index, to in ((0, n, up), (1, 55 + name[2], down)):
                    mine = strip(kind, section(kind, name[2]), parity, which)
                    start(mine, mine, index, to)
            else:
                unit, to, _ = route(at, name)
                start(view(kind, unit, name[-1]), view(kind, unit, name[-1]), n, to)

        for name in first:
            push(name)
        prepare()
        for n, name in enumerate(order):
            if name[1] == "z":
                for which, index, to in ((0, n, up), (1, 55 + name[2], down)):
                    got = strip(kind, section(kind, name[2]), 1 - parity, which)
                    remote(got, got, send.at[index], recv.at[index], to).wait_recv()
            else:
                got = view(kind, route(at, name)[2], name[-1])
                remote(got, got, send.at[n], recv.at[n], at.right).wait_recv()
            seen.add(name)
            for later in order:
                if name in needs(later) and seen.issuperset(needs(later)):
                    push(later)
            if n in over:
                i, q = over[n]
                got = handed(kind, section(kind, i), q)
                start(got, got, 70 + 15 * q + i, at.sib)
                tally(kind, section(kind, i), q)
        for c in sent:
            c.wait_send()

    def take(kind, order):
        for _, i, q in ends(kind, order):
            sec = section(kind, i)
            got = handed(kind, sec, q)
            remote(got, got, send.at[70 + 15 * q + i], recv.at[70 + 15 * q + i], at.sib).wait_recv()
            tally(kind, sec, q)

    sums[...] = jnp.zeros_like(sums)
    for kind in range(2):
        for q in range(2):
            tally(kind, at.me, q)
    pl.when(at.core == 0)(lambda: run(0, FIRST_A, ORDER_A))
    pl.when(at.core == 1)(lambda: run(1, FIRST_B, ORDER_B))
    pl.when(at.core == 1)(lambda: take(0, ORDER_A))
    pl.when(at.core == 0)(lambda: take(1, ORDER_B))


def grams(w, rows, raw, gg, mm):
    width = rows.shape[1]
    tile = lambda b: w[1, b * 8:(b + 1) * 8].reshape(256, width)

    def block(kind, _):
        for i in range(2):
            lhs = w[kind, i * 8:(i + 1) * 8].reshape(256, width)
            for b in range(i + 1):
                raw[2 * kind + i, :, b * 256:(b + 1) * 256] = dot(lhs, tile(b), NT)
            raw[2 * kind + i, :, 512:768] = dot(lhs, rows[...], NT)
        return 0

    lax.fori_loop(0, 2, block, 0)

    def keep(ref, g, first, value):
        hi, lo = halves(value)
        ref[g, first:first + value.shape[0], 0:128] = hi
        ref[g, first:first + value.shape[0], 128:256] = lo

    for i in range(4):
        for g in range(2 * (i % 2) + 2):
            keep(gg, g, i * 256, raw[i, :, g * 128:(g + 1) * 128])
    for g in range(2):
        for t in range(2):
            keep(gg, 2 + g, ALL + t * 128, raw[3, g * 128:(g + 1) * 128, t * 128:(t + 1) * 128].T)
    for j in range(4):
        for s in range(j + 1):
            keep(mm, j, s * 128, raw[j // 2, (j % 2) * 128:(j % 2 + 1) * 128, s * 128:(s + 1) * 128].T)


def chain(width, stat, row_sums, raw, gg, mm, u, v, c, acts, ds, fs, sc):
    for i in range(2):
        half = slice(i * 256, (i + 1) * 256)
        u[half] = raw[i, :, 640:768]
        v[half] = raw[2 + i, :, 640:768]
        c[half] = raw[2 + i, :, 512:640]

    for kind in range(2):
        for s in range(S):
            row_sums[kind, s] = jnp.broadcast_to(jnp.sum(row_sums[kind, s], axis=1, keepdims=True), (R, ROWS))

    def sums(kind, s):
        return row_sums[kind, s]

    def spot(a, s):
        o = s % 4
        parts = [jnp.zeros((o * R, ROWS), BF16)] * (o > 0) + [a] + [jnp.zeros(((3 - o) * R, ROWS), BF16)] * (o < 3)
        padded = jnp.concatenate(parts, axis=0) if len(parts) > 1 else a
        return jnp.concatenate([padded, padded], axis=0)

    total = lambda t: jnp.sum(t, axis=0, keepdims=True)
    mu, q = stat[0:1], stat[1:2]
    hid, slope, rstds, mus, kept, held = [], [], [], [], [], []
    for s in range(S):
        sl = slice(s * R, (s + 1) * R)
        rstd = lax.rsqrt(q * (1.0 / width) + 1e-5)
        h = rstd * (u[sl] - mu * sums(0, s))
        a, g = gelu_pair(h)
        a16 = a.astype(BF16)
        af = a16.astype(F32)
        acts[s] = a16
        old = v[sl]
        hid.append(h)
        slope.append(g)
        rstds.append(rstd)
        mus.append(mu)
        kept.append(old)
        held.append(af)
        if s < S - 1:
            rhs = spot(a16, s)
            wbs = sums(1, s)
            u[(s + 1) * R:] += dot(gg[s // 4, (s + 1) * R:ALL], rhs)
            new_v = v[s * R:] + dot(gg[s // 4, ALL + s * R:], rhs)
            v[s * R:] = new_v
            tot = total(af * wbs)
            q = q + total(af * (old + new_v[0:R] - (2.0 * mu) * wbs)) - tot * tot * (1.0 / width)
            q = jnp.maximum(q, 0.0)
            mu = mu + tot * (1.0 / width)
    cc, ee = jnp.zeros_like(mu), jnp.zeros_like(mu)
    blank = jnp.zeros((5, ROWS), F32)
    ds[S - 1] = jnp.zeros((R, ROWS), BF16)
    for j in range(S - 1, -1, -1):
        sl = slice(j * R, (j + 1) * R)
        sc[j] = jnp.concatenate([mus[j], cc, ee, blank], axis=0)
        da = c[sl] - cc * kept[j] - ee * sums(1, j)
        f16 = (rstds[j] * (da * slope[j])).astype(BF16)
        fs[j] = f16
        f = f16.astype(F32)
        a_j = total(f * sums(0, j)) * (1.0 / width)
        c_j = rstds[j] * total(f * hid[j]) * (1.0 / width)
        cc = cc + c_j
        ee = ee + a_j - c_j * mus[j]
        if j > 0:
            d16 = (held[j - 1] * cc).astype(BF16)
            ds[j - 1] = d16
            c[0:j * R] += dot(mm[j // 4, 0:j * R], spot(f16, j)) - dot(gg[(j - 1) // 4, ALL:ALL + j * R], spot(d16, j - 1))


def kernel(xd, xu, cd, cu, gain, wa, wb, tot,
           w, rows, stat, row_sums, raw, gg, mm, u, v, c, acts, ds, fs, sc, half, near, part, pieces, total,
           send, recv, rs_send, rs_recv, a2a_send, a2a_recv, ag_send, ag_recv, sh_send, sh_recv):
    at = Place()
    me, core, deep = at.me, at.core, at.deep
    width = rows.shape[1]
    step = width // deep
    far_first = sorted(range(deep), key=lambda d: (-min(d, deep - d), d))
    spots = [(k, e) for k in range(deep) for e in range(2) if (far_first[k], e) != (0, 0)]
    w[0, me] = (gain[...].astype(F32) * wa[...].astype(F32)).astype(BF16)
    w[1, me] = wb[...]
    greet([at.right, at.left, at.cross, at.sib] + [at.spot(far_first[k], e)[2] for k, e in spots])

    def prepare():
        for i, ref in enumerate((cd, cu, xd, xu)):
            for b in range(4):
                val = jnp.concatenate([ref[2 * b].astype(F32), ref[2 * b + 1].astype(F32)], axis=0)
                rows[i * 64 + b * 16:i * 64 + (b + 1) * 16] = val.astype(BF16)
        mus, qs = [], []
        for ref in (xd, xu):
            for b in range(8):
                val = ref[b].astype(F32)
                mean = jnp.sum(val, axis=1, keepdims=True) * (1.0 / width)
                val = val - mean
                mus.append(mean)
                qs.append(jnp.sum(val * val, axis=1, keepdims=True))
        wide = lambda t: jnp.broadcast_to(jnp.concatenate(t, axis=0), (ROWS, ROWS)).T[0:1]
        stat[0:1] = wide(mus)
        stat[1:2] = wide(qs)

    spread(at, w, row_sums, send, recv, prepare)
    grams(w, rows, raw, gg, mm)
    chain(width, stat, row_sums, raw, gg, mm, u, v, c, acts, ds, fs, sc)

    at_row = lax.broadcasted_iota(jnp.int32, (ALL, ROWS), 0)
    flat = lambda ref: ref[...].reshape(ALL, ROWS).astype(F32)
    turn = lambda t: t.T.astype(BF16)
    zx = turn(jnp.where(at_row < me * R, flat(acts), 0.0))
    zd = turn(jnp.where(at_row >= me * R, flat(ds), 0.0))
    fd = turn(jnp.where(at_row >= (me + 1) * R, flat(fs), 0.0))
    zxd = jnp.concatenate([zx, zd], axis=0)
    own = jnp.concatenate([sc[me], jnp.zeros((ROWS - 8, ROWS), F32)], axis=0).T
    mu, cc, ee = own[:, 0:1], own[:, 1:2], own[:, 2:3]
    act, f = acts[me], fs[me]

    def block(k):
        z = at.spot(far_first[k], 0)[1]
        cols = pl.ds(pl.multiple_of(z * step, step), step)
        from_b = dot(zxd, w[1, :, :, cols].reshape(ALL, step))
        x = rows[ROWS:, cols].astype(F32) + from_b[0:ROWS]
        dy = rows[0:ROWS, cols].astype(F32) + dot(fd, w[0, :, :, cols].reshape(ALL, step)) - from_b[ROWS:] - cc * x - ee
        half[k, 0:R] = dot(f, (x - mu).astype(BF16)).astype(BF16)
        half[k, R:] = dot(act, dy.astype(BF16)).astype(BF16)
        out = remote(half.at[k, pl.ds(pl.multiple_of((1 - core) * R, R), R)], near.at[k], rs_send.at[k], rs_recv.at[k], at.sib)
        out.start()
        return out

    def piece(k, e):
        y = at.y_lo if e == 0 else 1 - at.y_lo
        return part.at[k, pl.ds(pl.multiple_of(y * H, H), H)]

    out, moved = [], []
    for k in range(deep + 1):
        if k < deep:
            out.append(block(k))
        if k > 0:
            b = k - 1
            out[b].wait_recv()
            part[b] = (near[b].astype(F32) + half[b, pl.ds(pl.multiple_of(core * R, R), R)].astype(F32)).astype(BF16)
            for e in range(2):
                if (b, e) in spots:
                    n = 2 * b + e
                    moved.append(remote(piece(b, e), pieces.at[n], a2a_send.at[n], a2a_recv.at[n], at.spot(far_first[b], e)[2]))
                    moved[-1].start()
    acc = piece(far_first.index(0), 0)[...].astype(F32)
    for copy, (k, e) in zip(moved, spots):
        copy.wait_recv()
        acc = acc + pieces[2 * k + e].astype(F32)
    total[...] = acc.astype(BF16)

    def landing(kind, y, z):
        return tot.at[kind, pl.ds(pl.multiple_of(y * H, H), H), pl.ds(pl.multiple_of(z * step, step), step)]

    mine = landing(core, at.y_lo, at.z)
    for k, e in spots:
        n = 2 * k + e
        moved.append(remote(total, mine, ag_send.at[n], ag_recv.at[n], at.spot(far_first[k], e)[2]))
        moved[-1].start()
    mine[...] = total[...]
    moved.append(remote(mine, mine, sh_send.at[0], sh_recv.at[0], at.sib))
    moved[-1].start()
    came = [(at.y_lo, at.z)]
    for i, (k, e) in enumerate(spots):
        n = 2 * k + e
        y, z, to = at.spot(-far_first[k], e)
        got = landing(core, y, z)
        came.append((y, z))
        remote(got, got, ag_send.at[n], ag_recv.at[n], to).wait_recv()
        moved.append(remote(got, got, sh_send.at[1 + i], sh_recv.at[1 + i], at.sib))
        moved[-1].start()
    for i, (y, z) in enumerate(came):
        got = landing(1 - core, y, z)
        remote(got, got, sh_send.at[i], sh_recv.at[i], at.sib).wait_recv()
    for copy in out + moved:
        copy.wait_send()


def on_device(x_down, x_up, cot_down, cot_up, gain, w_a, w_b):
    width = x_down.shape[-1]
    deep = lax.axis_size("dp") // 4
    step = width // deep
    vmem = pl.BlockSpec(memory_space=pltpu.VMEM)
    sems = lambda n: [pltpu.SemaphoreType.DMA((n,)), pltpu.SemaphoreType.DMA((n,))]
    total = pl.pallas_call(
        kernel,
        out_shape=jax.ShapeDtypeStruct((2, R, width), BF16),
        in_specs=[vmem] * 7,
        out_specs=vmem,
        scratch_shapes=[
            pltpu.VMEM((2, S, R, width), BF16),
            pltpu.VMEM((2 * ROWS, width), BF16),
            pltpu.VMEM((8, ROWS), F32),
            pltpu.VMEM((2, S, R, ROWS), F32),
            pltpu.VMEM((4, 256, 768), F32),
            pltpu.VMEM((4, 2 * ALL, 256), BF16),
            pltpu.VMEM((4, ALL, 256), BF16),
            pltpu.VMEM((ALL, ROWS), F32),
            pltpu.VMEM((ALL, ROWS), F32),
            pltpu.VMEM((ALL, ROWS), F32),
            pltpu.VMEM((S, R, ROWS), BF16),
            pltpu.VMEM((S, R, ROWS), BF16),
            pltpu.VMEM((S, R, ROWS), BF16),
            pltpu.VMEM((S, 8, ROWS), F32),
            pltpu.VMEM((deep, 2 * R, step), BF16),
            pltpu.VMEM((deep, R, step), BF16),
            pltpu.VMEM((deep, R, step), BF16),
            pltpu.VMEM((2 * deep, H, step), BF16),
            pltpu.VMEM((H, step), BF16),
        ]
        + sems(100) + sems(deep) + sems(2 * deep) + sems(2 * deep) + sems(2 * deep),
        compiler_params=pltpu.CompilerParams(collective_id=0, has_side_effects=True, vmem_limit_bytes=56 * 2**20),
    )(x_down[0], x_up[0], cot_down[0], cot_up[0], gain, w_a[0], w_b[0])
    h = total[0].astype(F32)
    return jnp.sum(w_a[0].astype(F32) * h, axis=0)[None], (gain.astype(F32) * h)[None], total[1].astype(F32)[None]


def solution(mesh):
    data, held = P("dp", None, None, None), P("section", None, None)
    return jax.shard_map(
        on_device,
        mesh=mesh,
        in_specs=(data, data, data, data, P("section", None), held, held),
        out_specs=(P("section", None), held, held),
        check_vma=False,
    )
```

```python
import jax
import jax.numpy as jnp
from jax import lax
from jax.experimental import pallas as pl
from jax.experimental.pallas import tpu as pltpu
from jax.sharding import PartitionSpec as P

F32, BF16 = jnp.float32, jnp.bfloat16
S, R, H = 16, 32, 16
ALL = S * R
ROWS = 128
MESH = pl.DeviceIdType.MESH
NT = (((1,), (1,)), ((), ()))
NN = (((1,), (0,)), ((), ()))

FIRST_A = (
    (0, "xl", 0), (0, "xr", 0), (0, "xr", 1), (0, "y1", 0, 0), (0, "y1", 0, 1), (0, "xl", 1),
)
ORDER_A = (
    (0, "xr", 0), (0, "y1", 0, 0), (0, "xl", 0), (0, "xr", 1), (0, "y1", 0, 1), (0, "xl", 1),
    (0, "x2r", 0), (0, "y1", 1, 0), (0, "x2l", 0), (0, "y1", 2, 0), (0, "x2r", 1), (0, "y1", 1, 1),
    (0, "x2l", 1), (0, "z", 3), (0, "z", 6), (0, "y2", 0, 0), (0, "z", 0), (0, "y1", 2, 1),
    (0, "y2", 1, 0), (0, "y1", 3, 0), (0, "y2", 2, 0), (0, "y2", 0, 1), (0, "y2", 1, 1), (0, "y1", 3, 1),
    (0, "y2", 2, 1), (0, "y3", 1, 0), (0, "y2", 3, 0), (0, "z", 1), (0, "z", 7), (0, "y3", 0, 0),
    (0, "y3", 2, 0), (0, "y3", 1, 1), (0, "z", 12), (0, "y2", 3, 1), (0, "z", 4), (0, "y3", 3, 0),
    (0, "y4", 1, 0), (0, "y4", 0, 0), (0, "y3", 0, 1), (0, "y4", 2, 0), (0, "z", 9), (0, "y3", 2, 1),
    (0, "y4", 1, 1), (0, "y3", 3, 1), (0, "y4", 3, 0), (0, "z", 10), (0, "y4", 0, 1), (0, "z", 11),
    (0, "y4", 2, 1), (0, "z", 8), (0, "z", 5), (0, "y4", 3, 1), (0, "z", 2), (0, "z", 13),
    (0, "z", 14),
)
FIRST_B = (
    (1, "y1", 0), (1, "y1", 1), (1, "xr", 0, 0), (1, "xr", 0, 1), (1, "xl", 0, 0), (1, "xl", 0, 1),
)
ORDER_B = (
    (1, "y1", 0), (1, "xr", 0, 0), (1, "y1", 1), (1, "xl", 0, 0), (1, "xl", 0, 1), (1, "y2", 0),
    (1, "xr", 0, 1), (1, "xl", 1, 1), (1, "xl", 1, 0), (1, "y2", 1), (1, "xr", 1, 1), (1, "y3", 0),
    (1, "xr", 1, 0), (1, "xr", 2, 0), (1, "x2l", 1, 1), (1, "z", 0), (1, "xl", 2, 0), (1, "x2l", 0, 0),
    (1, "x2l", 0, 1), (1, "y3", 1), (1, "x2r", 0, 1), (1, "xr", 2, 1), (1, "z", 4), (1, "y4", 0),
    (1, "x2r", 0, 0), (1, "x2r", 1, 0), (1, "x2l", 2, 0), (1, "x2l", 1, 0), (1, "z", 3), (1, "y4", 1),
    (1, "x2r", 2, 0), (1, "xr", 3, 0), (1, "xl", 3, 0), (1, "xl", 2, 1), (1, "x2r", 1, 1), (1, "z", 5),
    (1, "xr", 3, 1), (1, "x2r", 3, 0), (1, "x2l", 3, 0), (1, "xl", 3, 1), (1, "x2l", 2, 1), (1, "z", 9),
    (1, "z", 13), (1, "z", 10), (1, "z", 2), (1, "x2r", 3, 1), (1, "z", 6), (1, "z", 8),
    (1, "z", 7), (1, "x2r", 2, 1), (1, "z", 12), (1, "z", 14), (1, "z", 11), (1, "x2l", 3, 1),
    (1, "z", 1),
)
BROUGHT = (
    [((0, "xr"),), ((0, "xl"),), ((0, "x2r"), (0, "x2l"))]
    + [b for t in range(4) for b in (((0, "y1", t),), ((0, "y2", t),), ((0, "y3", t), (0, "y4", t)))],
    [((1, "y1"),), ((1, "y2"),), ((1, "y3"), (1, "y4"))]
    + [b for r in range(4) for b in (((1, "xr", r),), ((1, "xl", r),), ((1, "x2r", r), (1, "x2l", r)))],
)


def dot(a, b, dims=NN):
    return lax.dot_general(a, b, dims, preferred_element_type=F32)


def gelu_pair(h):
    k = 0.7978845608028654
    t = jnp.tanh(k * (h + 0.044715 * h * h * h))
    up = 0.5 * (1.0 + t)
    return h * up, up + 0.5 * h * (1.0 - t * t) * (k * (1.0 + 3 * 0.044715 * h * h))


def halves(m):
    hi = m.astype(BF16)
    return hi, (m - hi.astype(F32)).astype(BF16)


class Place:
    def __init__(self):
        self.me, self.dp = lax.axis_index("section"), lax.axis_index("dp")
        self.deep = lax.axis_size("dp") // 4
        self.p, self.x = self.me // 4, lax.rem(self.me, 4)
        self.core = lax.rem(self.dp, 2)
        self.z = lax.rem(self.dp // 2, self.deep)
        self.y_lo = self.dp // (2 * self.deep)
        self.sgn = 2 * self.y_lo - 1
        other = self.dp + (1 - 2 * self.y_lo) * (2 * self.deep)
        self.right, self.left = (self.p * 4 + self.col(1), self.dp), (self.p * 4 + self.col(-1), self.dp)
        self.cross, self.pair = (self.row(self.sgn) * 4 + self.x, other), (self.me, other)
        self.sib = (self.me, self.dp + 1 - 2 * self.core)

    def row(self, d):
        return lax.rem(self.p + d + 4, 4)

    def col(self, d):
        return lax.rem(self.x + d + 4, 4)

    def spot(self, d, e):
        y = self.y_lo if e == 0 else 1 - self.y_lo
        z = lax.rem(self.z + d + self.deep, self.deep)
        return y, z, (self.me, (y * self.deep + z) * 2 + self.core)


def greet(partners, meanwhile):
    barrier = pltpu.get_barrier_semaphore()
    for partner in partners:
        pl.semaphore_signal(barrier, inc=1, device_id=partner, device_id_type=MESH)
    meanwhile()
    pl.semaphore_wait(barrier, len(partners))


def remote(src, dst, send, recv, to):
    return pltpu.make_async_remote_copy(src_ref=src, dst_ref=dst, send_sem=send, recv_sem=recv, device_id=to, device_id_type=MESH)


def route(at, name):
    p, x, y = at.p, at.x, at.y_lo
    near, away, far = at.row(at.sgn), at.row(-at.sgn), at.row(2)
    lft, rgt, opp = at.col(-1), at.col(1), at.col(2)
    kind, what = name[0], name[1]
    if what[0] == "x":
        r = (p, near, away, far)[name[2] if kind else 0] * 4
        return {
            "xr": ((r + x, None), at.right, (r + lft, None)),
            "xl": ((r + x, None), at.left, (r + rgt, None)),
            "x2r": ((r + lft, y), at.right, (r + opp, y)),
            "x2l": ((r + rgt, 1 - y), at.left, (r + opp, 1 - y)),
        }[what]
    t = x if kind else (x, lft, rgt, opp)[name[2]]
    return {
        "y1": ((p * 4 + t, None), at.cross, (near * 4 + t, None)),
        "y2": ((near * 4 + t, None), at.pair, (away * 4 + t, None)),
        "y3": ((away * 4 + t, y), at.cross, (far * 4 + t, 1 - y)),
        "y4": ((far * 4 + t, 1 - y), at.pair, (far * 4 + t, y)),
    }[what]


def needs(name):
    kind, what, rest, q = name[0], name[1], name[2:-1], name[-1:]
    if what == "z":
        return [base + (0,) for base in BROUGHT[kind][name[2]]]
    if what in ("x2r", "x2l"):
        return [(kind, "xr" if what == "x2r" else "xl") + rest + q]
    if what in ("y2", "y3", "y4"):
        return [(kind, {"y2": "y1", "y3": "y2", "y4": "y3"}[what]) + rest + q]
    if kind == 0 and what == "y1":
        return [[], [(0, "xr") + q], [(0, "xl") + q], [(0, "x2r") + q, (0, "x2l") + q]][rest[0]]
    if kind == 1 and what in ("xr", "xl"):
        return [[], [(1, "y1") + q], [(1, "y2") + q], [(1, "y3") + q, (1, "y4") + q]][rest[0]]
    return []


def sum_tiles(w, sec, first, last):
    acc = w[1, sec, :, first:first + 128].astype(F32)
    for col in range(first + 128, last, 128):
        acc = acc + w[1, sec, :, col:col + 128].astype(F32)
    return acc


def spread(at, w, sums, send, recv, prepare):
    width = w.shape[-1]
    part = width // 128 * 3 // 10 * 128
    parity = lax.rem(at.z, 2)
    up, down = at.spot(1, 0)[2], at.spot(-1, 0)[2]

    def view(kind, unit, q):
        rows = pl.ds(0, R) if unit[1] is None else pl.ds(pl.multiple_of(unit[1] * H, H), H)
        cols = pl.ds(2 * part, width - 2 * part) if q else pl.ds(pl.multiple_of(parity * part, 128), part)
        return w.at[kind, unit[0], rows, cols]

    def strip(kind, sec, side, which):
        start = side * part + which * (part // 2)
        return w.at[kind, sec, :, pl.ds(pl.multiple_of(start, 128), part // 2)]

    def handed(kind, sec, q):
        return w.at[kind, sec, :, pl.ds(2 * part, width - 2 * part) if q else pl.ds(0, 2 * part)]

    def tally(sec, q):
        sums[sec] += sum_tiles(w, sec, 2 * part if q else 0, width if q else 2 * part)

    def section(kind, i):
        return route(at, BROUGHT[kind][i][0])[2][0]

    def ends(kind, order):
        found = []
        for n, name in enumerate(order):
            if name[1] == "z":
                found.append((n, name[2], 0))
            elif name[-1] == 1:
                for i, bases in enumerate(BROUGHT[kind]):
                    if name[:-1] in bases and all(order.index(base + (1,)) <= n for base in bases):
                        found.append((n, i, 1))
        return found

    def run(kind, first, order):
        sent, seen = [], set()
        over = {n: (i, q) for n, i, q in ends(kind, order)}

        def start(src, dst, index, to):
            c = remote(src, dst, send.at[index], recv.at[index], to)
            c.start()
            sent.append(c)

        def push(name):
            n = order.index(name)
            if name[1] == "z":
                for which, index, to in ((0, n, up), (1, 55 + name[2], down)):
                    mine = strip(kind, section(kind, name[2]), parity, which)
                    start(mine, mine, index, to)
            else:
                unit, to, _ = route(at, name)
                start(view(kind, unit, name[-1]), view(kind, unit, name[-1]), n, to)

        for name in first:
            push(name)
        prepare()
        if kind:
            sums[...] = jnp.zeros_like(sums)
            sums[at.me] = sum_tiles(w, at.me, 0, width)
        for n, name in enumerate(order):
            if name[1] == "z":
                for which, index, to in ((0, n, up), (1, 55 + name[2], down)):
                    got = strip(kind, section(kind, name[2]), 1 - parity, which)
                    remote(got, got, send.at[index], recv.at[index], to).wait_recv()
            else:
                got = view(kind, route(at, name)[2], name[-1])
                remote(got, got, send.at[n], recv.at[n], at.right).wait_recv()
            seen.add(name)
            for later in order:
                if name in needs(later) and seen.issuperset(needs(later)):
                    push(later)
            if n in over:
                i, q = over[n]
                got = handed(kind, section(kind, i), q)
                start(got, got, 70 + 15 * q + i, at.sib)
                if kind:
                    tally(section(kind, i), q)
        if kind:
            start(sums, sums, 100, at.sib)
        for c in sent:
            c.wait_send()

    def take(kind, order):
        for _, i, q in ends(kind, order):
            sec = section(kind, i)
            got = handed(kind, sec, q)
            remote(got, got, send.at[70 + 15 * q + i], recv.at[70 + 15 * q + i], at.sib).wait_recv()

    pl.when(at.core == 0)(lambda: run(0, FIRST_A, ORDER_A))
    pl.when(at.core == 1)(lambda: run(1, FIRST_B, ORDER_B))
    pl.when(at.core == 1)(lambda: take(0, ORDER_A))
    pl.when(at.core == 0)(lambda: take(1, ORDER_B))
    pl.when(at.core == 0)(lambda: remote(sums, sums, send.at[100], recv.at[100], at.sib).wait_recv())


def grams(w, rows, raw, gg, mm):
    width = rows.shape[1]
    tile = lambda b: w[1, b * 8:(b + 1) * 8].reshape(256, width)

    def block(kind, _):
        beside = rows.at[pl.ds(pl.multiple_of((1 - kind) * ROWS, ROWS), 2 * ROWS)]
        for i in range(2):
            lhs = w[kind, i * 8:(i + 1) * 8].reshape(256, width)
            for b in range(i + 1):
                raw[2 * kind + i, :, b * 256:(b + 1) * 256] = dot(lhs, tile(b), NT)
            raw[2 * kind + i, :, 512:768] = dot(lhs, beside[...], NT)
        return 0

    lax.fori_loop(0, 2, block, 0)

    def keep(ref, g, first, value):
        hi, lo = halves(value)
        ref[g, first:first + value.shape[0], 0:128] = hi
        ref[g, first:first + value.shape[0], 128:256] = lo

    for i in range(4):
        for g in range(2 * (i % 2) + 2):
            keep(gg, g, i * 256, raw[i, :, g * 128:(g + 1) * 128])
    for g in range(2):
        for t in range(2):
            keep(gg, 2 + g, ALL + t * 128, raw[3, g * 128:(g + 1) * 128, t * 128:(t + 1) * 128].T)
    for j in range(4):
        for s in range(j + 1):
            keep(mm, j, s * 128, raw[j // 2, (j % 2) * 128:(j % 2 + 1) * 128, s * 128:(s + 1) * 128].T)


def chain(width, stat, row_sums, wide, raw, gg, mm, u, v, c, acts, ds, fs, sc):
    for i in range(2):
        half = slice(i * 256, (i + 1) * 256)
        u[half] = raw[i, :, 512:640]
        v[half] = raw[2 + i, :, 640:768]
        c[half] = raw[2 + i, :, 512:640]

    for s in range(S):
        wide[s] = jnp.broadcast_to(jnp.sum(row_sums[s], axis=1, keepdims=True), (R, ROWS))

    def sums(kind, s):
        return wide[s] if kind else raw[s // 8, (s % 8) * R:(s % 8 + 1) * R, 640:768]

    def spot(a, s):
        o = s % 4
        parts = [jnp.zeros((o * R, ROWS), BF16)] * (o > 0) + [a] + [jnp.zeros(((3 - o) * R, ROWS), BF16)] * (o < 3)
        padded = jnp.concatenate(parts, axis=0) if len(parts) > 1 else a
        return jnp.concatenate([padded, padded], axis=0)

    total = lambda t: jnp.sum(t, axis=0, keepdims=True)
    mu, q = stat[0:1], stat[1:2]
    hid, slope, rstds, mus, kept, held = [], [], [], [], [], []
    for s in range(S):
        sl = slice(s * R, (s + 1) * R)
        rstd = lax.rsqrt(q * (1.0 / width) + 1e-5)
        h = rstd * (u[sl] - mu * sums(0, s))
        a, g = gelu_pair(h)
        a16 = a.astype(BF16)
        af = a16.astype(F32)
        acts[s] = a16
        old = v[sl]
        hid.append(h)
        slope.append(g)
        rstds.append(rstd)
        mus.append(mu)
        kept.append(old)
        held.append(af)
        if s < S - 1:
            rhs = spot(a16, s)
            wbs = sums(1, s)
            u[(s + 1) * R:] += dot(gg[s // 4, (s + 1) * R:ALL], rhs)
            new_v = v[s * R:] + dot(gg[s // 4, ALL + s * R:], rhs)
            v[s * R:] = new_v
            tot = total(af * wbs)
            q = q + total(af * (old + new_v[0:R] - (2.0 * mu) * wbs)) - tot * tot * (1.0 / width)
            q = jnp.maximum(q, 0.0)
            mu = mu + tot * (1.0 / width)
    cc, ee = jnp.zeros_like(mu), jnp.zeros_like(mu)
    blank = jnp.zeros((5, ROWS), F32)
    ds[S - 1] = jnp.zeros((R, ROWS), BF16)
    for j in range(S - 1, -1, -1):
        sl = slice(j * R, (j + 1) * R)
        sc[j] = jnp.concatenate([mus[j], cc, ee, blank], axis=0)
        da = c[sl] - cc * kept[j] - ee * sums(1, j)
        f16 = (rstds[j] * (da * slope[j])).astype(BF16)
        fs[j] = f16
        f = f16.astype(F32)
        a_j = total(f * sums(0, j)) * (1.0 / width)
        c_j = rstds[j] * total(f * hid[j]) * (1.0 / width)
        cc = cc + c_j
        ee = ee + a_j - c_j * mus[j]
        if j > 0:
            d16 = (held[j - 1] * cc).astype(BF16)
            ds[j - 1] = d16
            c[0:j * R] += dot(mm[j // 4, 0:j * R], spot(f16, j)) - dot(gg[(j - 1) // 4, ALL:ALL + j * R], spot(d16, j - 1))


def kernel(xd, xu, cd, cu, gain, wa, wb, out_ref, gg_out,
           w, data, rows, stat, row_sums, wide, raw, gg, mm, u, v, c, acts, ds, fs, sc, half, near, part, pieces, beside, merged, total, tot,
           local, send, recv, rs_send, rs_recv, pr_send, pr_recv, a2a_send, a2a_recv, ag_send, ag_recv, sh_send, sh_recv):
    at = Place()
    me, core, deep = at.me, at.core, at.deep
    width = rows.shape[1]
    step = width // deep
    hops = lambda d: min(d, deep - d)
    far_first = sorted(range(deep), key=lambda d: (-hops(d), d))
    distant = [k for k in range(deep) if hops(far_first[k]) >= max(1, deep * 3 // 8)]
    spots = [(k, e) for k in range(deep) for e in range(2) if (far_first[k], e) != (0, 0)]
    loads = [pltpu.make_async_copy(ref, data.at[i], local.at[i]) for i, ref in enumerate((cd, cu, xd, xu))]
    for load in loads:
        load.start()

    def own():
        w[0, me] = (gain[...].astype(F32) * wa[...].astype(F32)).astype(BF16)
        w[1, me] = wb[...]

    greet([at.right, at.left, at.cross, at.sib] + [at.spot(far_first[k], e)[2] for k, e in spots], own)

    def prepare():
        for load in loads:
            load.wait()
        rows[2 * ROWS:] = jnp.ones((ROWS, width), BF16)
        for i in range(4):
            for b in range(4):
                val = jnp.concatenate([data[i, 2 * b].astype(F32), data[i, 2 * b + 1].astype(F32)], axis=0)
                rows[i * 64 + b * 16:i * 64 + (b + 1) * 16] = val.astype(BF16)
        mus, qs = [], []
        for i in (2, 3):
            for b in range(8):
                val = data[i, b].astype(F32)
                mean = jnp.sum(val, axis=1, keepdims=True) * (1.0 / width)
                val = val - mean
                mus.append(mean)
                qs.append(jnp.sum(val * val, axis=1, keepdims=True))
        wide = lambda t: jnp.broadcast_to(jnp.concatenate(t, axis=0), (ROWS, ROWS)).T[0:1]
        stat[0:1] = wide(mus)
        stat[1:2] = wide(qs)

    spread(at, w, row_sums, send, recv, prepare)
    grams(w, rows, raw, gg, mm)
    chain(width, stat, row_sums, wide, raw, gg, mm, u, v, c, acts, ds, fs, sc)

    at_row = lax.broadcasted_iota(jnp.int32, (ALL, ROWS), 0)
    flat = lambda ref: ref[...].reshape(ALL, ROWS).astype(F32)
    turn = lambda t: t.T.astype(BF16)
    zx = turn(jnp.where(at_row < me * R, flat(acts), 0.0))
    zd = turn(jnp.where(at_row >= me * R, flat(ds), 0.0))
    fd = turn(jnp.where(at_row >= (me + 1) * R, flat(fs), 0.0))
    zxd = jnp.concatenate([zx, zd], axis=0)
    own = jnp.concatenate([sc[me], jnp.zeros((ROWS - 8, ROWS), F32)], axis=0).T
    mu, cc, ee = own[:, 0:1], own[:, 1:2], own[:, 2:3]
    act, f = acts[me], fs[me]

    def block(k):
        z = at.spot(far_first[k], 0)[1]
        cols = pl.ds(pl.multiple_of(z * step, step), step)
        from_b = dot(zxd, w[1, :, :, cols].reshape(ALL, step))
        x = rows[ROWS:2 * ROWS, cols].astype(F32) + from_b[0:ROWS]
        dy = rows[0:ROWS, cols].astype(F32) + dot(fd, w[0, :, :, cols].reshape(ALL, step)) - from_b[ROWS:] - cc * x - ee
        half[k, 0:R] = dot(f, (x - mu).astype(BF16)).astype(BF16)
        half[k, R:] = dot(act, dy.astype(BF16)).astype(BF16)
        out = remote(half.at[k, pl.ds(pl.multiple_of((1 - core) * R, R), R)], near.at[k], rs_send.at[k], rs_recv.at[k], at.sib)
        out.start()
        return out

    def piece(k, e):
        y = at.y_lo if e == 0 else 1 - at.y_lo
        return part.at[k, pl.ds(pl.multiple_of(y * H, H), H)]

    out, moved, swaps, came = [], [], {}, []

    def give(b, e, src):
        n = 2 * b + e
        came.append(remote(src, pieces.at[n], a2a_send.at[n], a2a_recv.at[n], at.spot(far_first[b], e)[2]))
        came[-1].start()

    def settle(b):
        out[b].wait_recv()
        part[b] = (near[b].astype(F32) + half[b, pl.ds(pl.multiple_of(core * R, R), R)].astype(F32)).astype(BF16)
        if b in distant:
            n = distant.index(b)
            swaps[b] = remote(piece(b, 1), beside.at[n], pr_send.at[n], pr_recv.at[n], at.pair)
            swaps[b].start()
        else:
            for e in range(2):
                if (b, e) in spots:
                    give(b, e, piece(b, e))

    def forward(b):
        n = distant.index(b)
        swaps[b].wait_recv()
        merged[n] = (beside[n].astype(F32) + piece(b, 0)[...].astype(F32)).astype(BF16)
        give(b, 0, merged.at[n])

    lag = min(4, deep - 1)
    for k in range(deep + 1):
        if k < deep:
            out.append(block(k))
        if k > 0:
            settle(k - 1)
        if k - 1 - lag in distant:
            forward(k - 1 - lag)
    for b in distant:
        if b + 1 + lag > deep:
            forward(b)
    acc = piece(far_first.index(0), 0)[...].astype(F32)
    order = [(k, e) for k, e in spots if k not in distant] + [(k, 0) for k in distant]
    for k, e in order:
        n = 2 * k + e
        remote(total, pieces.at[n], a2a_send.at[n], a2a_recv.at[n], at.pair).wait_recv()
        acc = acc + pieces[n].astype(F32)
    total[...] = acc.astype(BF16)

    def landing(kind, y, z):
        return tot.at[kind, pl.ds(pl.multiple_of(y * H, H), H), pl.ds(pl.multiple_of(z * step, step), step)]

    mine = landing(core, at.y_lo, at.z)
    for k, e in spots:
        if k not in distant or e == 0:
            n = 2 * k + e
            moved.append(remote(total, mine, ag_send.at[n], ag_recv.at[n], at.spot(far_first[k], e)[2]))
            moved[-1].start()
    mine[...] = total[...]
    shared = []

    def share(y, z):
        got = landing(core, y, z)
        shared.append((y, z))
        moved.append(remote(got, got, sh_send.at[len(shared) - 1], sh_recv.at[len(shared) - 1], at.sib))
        moved[-1].start()

    share(at.y_lo, at.z)
    order = [(k, 0) for k in distant] + [(k, e) for k, e in reversed(spots) if k not in distant] + [(k, 1) for k in distant]
    for k, e in order:
        n = 2 * k + e
        y, z, _ = at.spot(-far_first[k], e)
        got = landing(core, y, z)
        remote(got, got, ag_send.at[n], ag_recv.at[n], at.pair).wait_recv()
        if k in distant and e == 0:
            moved.append(remote(got, got, ag_send.at[n + 1], ag_recv.at[n + 1], at.pair))
            moved[-1].start()
        share(y, z)
    for i, (y, z) in enumerate(shared):
        got = landing(1 - core, y, z)
        remote(got, got, sh_send.at[i], sh_recv.at[i], at.sib).wait_recv()
    for i in range(width // ROWS):
        cols = slice(i * ROWS, (i + 1) * ROWS)
        h = tot[0, :, cols].astype(F32)
        out_ref[0:R, cols] = gain[:, cols].astype(F32) * h
        out_ref[R:, cols] = tot[1, :, cols].astype(F32)
        product = wa[:, cols].astype(F32) * h
        gg_out[i:i + 1] = jnp.sum(product[0:H], axis=0, keepdims=True)
        gg_out[width // ROWS + i:width // ROWS + i + 1] = jnp.sum(product[H:], axis=0, keepdims=True)
    for copy in out + came + list(swaps.values()) + moved:
        copy.wait_send()


def on_device(x_down, x_up, cot_down, cot_up, gain, w_a, w_b):
    width = x_down.shape[-1]
    deep = lax.axis_size("dp") // 4
    step = width // deep
    vmem = pl.BlockSpec(memory_space=pltpu.VMEM)
    sems = lambda n: [pltpu.SemaphoreType.DMA((n,)), pltpu.SemaphoreType.DMA((n,))]
    far = max(1, len([d for d in range(deep) if min(d, deep - d) >= max(1, deep * 3 // 8)]))
    total, gg = pl.pallas_call(
        kernel,
        out_shape=(jax.ShapeDtypeStruct((2 * R, width), F32), jax.ShapeDtypeStruct((2 * (width // ROWS), ROWS), F32)),
        in_specs=[pl.BlockSpec(memory_space=pl.ANY)] * 4 + [vmem] * 3,
        out_specs=(vmem, vmem),
        scratch_shapes=[
            pltpu.VMEM((2, S, R, width), BF16),
            pltpu.VMEM((4, 8, 8, width), BF16),
            pltpu.VMEM((3 * ROWS, width), BF16),
            pltpu.VMEM((8, ROWS), F32),
            pltpu.VMEM((S, R, ROWS), F32),
            pltpu.VMEM((S, R, ROWS), F32),
            pltpu.VMEM((4, 256, 768), F32),
            pltpu.VMEM((4, 2 * ALL, 256), BF16),
            pltpu.VMEM((4, ALL, 256), BF16),
            pltpu.VMEM((ALL, ROWS), F32),
            pltpu.VMEM((ALL, ROWS), F32),
            pltpu.VMEM((ALL, ROWS), F32),
            pltpu.VMEM((S, R, ROWS), BF16),
            pltpu.VMEM((S, R, ROWS), BF16),
            pltpu.VMEM((S, R, ROWS), BF16),
            pltpu.VMEM((S, 8, ROWS), F32),
            pltpu.VMEM((deep, 2 * R, step), BF16),
            pltpu.VMEM((deep, R, step), BF16),
            pltpu.VMEM((deep, R, step), BF16),
            pltpu.VMEM((2 * deep, H, step), BF16),
            pltpu.VMEM((far, H, step), BF16),
            pltpu.VMEM((far, H, step), BF16),
            pltpu.VMEM((H, step), BF16),
            pltpu.VMEM((2, R, width), BF16),
            pltpu.SemaphoreType.DMA((4,)),
        ]
        + sems(101) + sems(deep) + sems(far) + sems(2 * deep) + sems(2 * deep) + sems(2 * deep),
        compiler_params=pltpu.CompilerParams(collective_id=0, has_side_effects=True, vmem_limit_bytes=56 * 2**20),
    )(x_down[0], x_up[0], cot_down[0], cot_up[0], gain, w_a[0], w_b[0])
    gg = lax.optimization_barrier(gg[:width // ROWS] + gg[width // ROWS:])
    return gg.reshape(1, width), total[:R][None], total[R:][None]


def solution(mesh):
    data, held = P("dp", None, None, None), P("section", None, None)
    return jax.shard_map(
        on_device,
        mesh=mesh,
        in_specs=(data, data, data, data, P("section", None), held, held),
        out_specs=(P("section", None), held, held),
        check_vma=False,
    )
```
